32 devices in a mesh: gx: 8 (over z, x), gy: 4 (over y, core).
Axes of the slice: x: 2, y: 2, z: 4, core: 2. Of those that a mesh axis runs over, the one named last changes fastest.
Arguments:
- rhs_field: float32 [64, 32, 128], P('gx', 'gy'), may hold values from -6 to 6
- accumulation: float32 [64, 32, 128], P('gx', 'gy'), may hold values from 0.05 to 0.5
- trans_x: float32 [64, 32, 128], P('gx', 'gy'), may hold values from 0.1 to 10
- trans_y: float32 [64, 32, 128], P('gx', 'gy'), may hold values from 0.1 to 10
- trans_z: float32 [64, 32, 128], P('gx', 'gy'), may hold values from 0.02 to 2
- held_cells: int32 [4, 8, 8, 128], P(None, 'gx', 'gy'), may hold values from 0 to 8191
- perf_host: int32 [8, 8, 128], P('gx', 'gy'), may hold values from 0 to 3, as said below
- well_index: float32 [8, 8, 128], P('gx', 'gy'), may hold values from 0.1 to 2
- seg_cond: float32 [8, 8, 128], P('gx', 'gy'), may hold values from 0.5 to 4
- seg_rate: float32 [8, 8, 128], P('gx', 'gy'), may hold values from -6 to 6
Outputs:
- pressure: float32 [64, 32, 128], P('gx', 'gy')
- seg_pressure: float32 [8, 8, 128], P('gx', 'gy')
The draws below stay inside these ranges and needn't reach their ends.
Inputs may be any that keep to these rules, and one draw needn't show every extreme that they name: `held_cells`: local cell numbers, x-major then y then layer. `perf_host`: nondecreasing along a well's slots, starting at 0 in slot 0 and ending at 3 in the last slot: the perforations on each device form one run of slots.
All inputs are finite; a program needn't handle non-finite values.
Results may differ from the reference program's by a relative error of at most 0.00002.
Values sent between devices are 32-bit elements; how exact they have to be, the bound alone decides.
A program may use at most 64 MiB of HBM per device.

```python
import math
import jax
import jax.numpy as jnp

CX = 8
CY = 8
CZ = 128
W_DEV = 2
PERF = 128
REACH = 4
SWEEPS = 6
NX = 64
NY = 32
WROWS = 8
N_GX = 8
N_GY = 4


def draw_perf_host(key, part):
    cuts = jax.random.randint(key, (N_GX, WROWS, REACH - 1), 1, PERF)
    slot = jnp.arange(PERF, dtype=jnp.int32)
    above = (slot[None, None, None, :] >= cuts[:, :, :, None]).astype(jnp.int32)
    return jnp.sum(above, axis=2).astype(jnp.int32)


def touch_ends(result, stream_key, low, top_value):
    extent = result.shape
    index_at = [jax.random.randint(jax.random.fold_in(stream_key, axis), (), 0, extent[axis]) for axis in range(len(extent))]
    result = result.at[tuple(index_at)].set(low)
    longest = extent.index(max(extent))
    index_at[longest] = (index_at[longest] + 1) % extent[longest]
    return result.at[tuple(index_at)].set(top_value)


def level_of(own_key, dims, split, low, top_value):
    def one(axis_at, parts):
        steps = jax.random.uniform(jax.random.fold_in(jax.random.fold_in(own_key, 6), axis_at), (parts,), jnp.float32, low / len(split), top_value / len(split))
        return jnp.repeat(jnp.exp(steps), dims[axis_at] // parts).reshape((-1,) + (1,) * (len(dims) - axis_at - 1))

    factor_of = one(*split[0])
    for cut in split[1:]:
        factor_of = factor_of * one(*cut)
    return factor_of


def noise(rng, dims, spread, most, pieces=(), kind=jnp.bfloat16):
    values = spread * jax.random.normal(rng, dims, jnp.float32)
    if pieces:
        values = values * level_of(rng, dims, pieces, -0.22, 0.18)
    return jnp.clip(values, -most, most).astype(kind)


def setup_inputs(seed: int = 0) -> dict:
    keys = jax.random.split(jax.random.key(seed), 11)
    rhs_field = noise(keys[0], (NX, NY, CZ), 1.0, 6.0, ((0, 8), (1, 4)), jnp.float32)
    accumulation = jnp.clip(jnp.exp(math.log(0.5) - 2.3025851 * jax.random.uniform(keys[1], (NX, NY, CZ), jnp.float32) ** level_of(keys[1], (NX, NY, CZ), ((0, 8), (1, 4)), -0.2, 0.2)), 0.05, 0.5)
    trans_x = jnp.clip(jnp.exp(math.log(10.0) - 4.6051702 * jax.random.uniform(keys[2], (NX, NY, CZ), jnp.float32) ** level_of(keys[2], (NX, NY, CZ), ((0, 8), (1, 4)), -0.2, 0.2)), 0.1, 10.0)
    trans_y = jnp.clip(jnp.exp(math.log(10.0) - 4.6051702 * jax.random.uniform(keys[3], (NX, NY, CZ), jnp.float32) ** level_of(keys[3], (NX, NY, CZ), ((0, 8), (1, 4)), -0.2, 0.2)), 0.1, 10.0)
    trans_z = jnp.clip(jnp.exp(math.log(2.0) - 4.6051702 * jax.random.uniform(keys[4], (NX, NY, CZ), jnp.float32) ** level_of(keys[4], (NX, NY, CZ), ((0, 8), (1, 4)), -0.2, 0.2)), 0.02, 2.0)
    held_cells = touch_ends(jax.random.randint(keys[5], (REACH, N_GX, WROWS, PERF), 0, CX * CY * CZ), jax.random.fold_in(keys[5], 1), 0, (CX * CY * CZ) - 1).astype(jnp.int32)
    perf_host = draw_perf_host(jax.random.fold_in(keys[10], 71), 0)
    well_index = jnp.clip(jnp.exp(math.log(2.0) - 2.9957323 * jax.random.uniform(keys[7], (N_GX, WROWS, PERF), jnp.float32) ** level_of(keys[7], (N_GX, WROWS, PERF), ((0, 8), (1, 4)), -0.2, 0.2)), 0.1, 2.0)
    seg_cond = jnp.clip(jnp.exp(math.log(4.0) - 2.0794415 * jax.random.uniform(keys[8], (N_GX, WROWS, PERF), jnp.float32) ** level_of(keys[8], (N_GX, WROWS, PERF), ((0, 8), (1, 4)), -0.2, 0.2)), 0.5, 4.0)
    seg_rate = noise(keys[9], (N_GX, WROWS, PERF), 1.0, 6.0, ((0, 8), (1, 4)), jnp.float32)
    return {"rhs_field": rhs_field, "accumulation": accumulation, "trans_x": trans_x, "trans_y": trans_y, "trans_z": trans_z, "held_cells": held_cells, "perf_host": perf_host, "well_index": well_index, "seg_cond": seg_cond, "seg_rate": seg_rate}


def moved_up(field, axis):
    size = field.shape[axis]
    head = jnp.zeros_like(jax.lax.slice_in_dim(field, 0, 1, axis=axis))
    return jnp.concatenate([head, jax.lax.slice_in_dim(field, 0, size - 1, axis=axis)], axis=axis)


def to_local(field):
    return field.reshape(N_GX, CX, N_GY, CY, CZ).transpose(0, 2, 1, 3, 4).reshape(N_GX, N_GY, CX * CY * CZ)


def from_local(blocks):
    return blocks.reshape(N_GX, N_GY, CX, CY, CZ).transpose(0, 2, 1, 3, 4).reshape(NX, NY, CZ)


def reference(rhs_field, accumulation, trans_x, trans_y, trans_z, held_cells, perf_host, well_index, seg_cond, seg_rate):
    wx = moved_up(trans_x, 0)
    wy = moved_up(trans_y, 1)
    wz = moved_up(trans_z, 2)
    diag = accumulation + trans_x + wx + trans_y + wy + trans_z + wz
    slot = jnp.arange(PERF)
    fm = jnp.where(slot[None, None, :] > 0, seg_cond, jnp.float32(0.0))
    fp = jnp.concatenate([fm[:, :, 1:], jnp.zeros_like(fm[:, :, :1])], axis=2)
    held = held_cells.reshape(REACH, N_GX, N_GY, W_DEV * PERF)
    pressure = jnp.zeros_like(rhs_field)
    seg_pressure = jnp.zeros_like(seg_rate)
    row_x = jnp.arange(N_GX)[:, None, None]
    row_y = jnp.arange(N_GY)[None, :, None]
    for sweep in range(SWEEPS):
        blocks = to_local(pressure)
        cell_p = jnp.zeros_like(seg_rate)
        for r in range(REACH):
            values = jnp.take_along_axis(blocks, held[r], axis=2).reshape(N_GX, WROWS, PERF)
            values = jnp.roll(values, -r, axis=0)
            cell_p = cell_p + jnp.where(perf_host == r, values, jnp.float32(0.0))
        seg_prev = jnp.concatenate([jnp.zeros_like(seg_pressure[:, :, :1]), seg_pressure[:, :, :-1]], axis=2)
        seg_next = jnp.concatenate([seg_pressure[:, :, 1:], jnp.zeros_like(seg_pressure[:, :, :1])], axis=2)
        seg_res = seg_rate - (well_index * (seg_pressure - cell_p) + fm * (seg_pressure - seg_prev) + fp * (seg_pressure - seg_next))
        seg_pressure = seg_pressure + 0.8 * seg_res / (well_index + fm + fp)
        flux = well_index * (cell_p - seg_pressure)
        term_blocks = jnp.zeros_like(blocks)
        for r in range(REACH):
            sent = jnp.roll(jnp.where(perf_host == r, flux, jnp.float32(0.0)), r, axis=0)
            term_blocks = term_blocks.at[row_x, row_y, held[r]].add(sent.reshape(N_GX, N_GY, W_DEV * PERF))
        well_term = from_local(term_blocks)
        padded = jnp.pad(pressure, 1)
        core = padded[1:-1, 1:-1, 1:-1]
        applied = accumulation * pressure
        applied = applied + trans_x * (core - padded[2:, 1:-1, 1:-1]) + wx * (core - padded[:-2, 1:-1, 1:-1])
        applied = applied + trans_y * (core - padded[1:-1, 2:, 1:-1]) + wy * (core - padded[1:-1, :-2, 1:-1])
        applied = applied + trans_z * (core - padded[1:-1, 1:-1, 2:]) + wz * (core - padded[1:-1, 1:-1, :-2])
        pressure = pressure + 0.7 * (rhs_field - applied - well_term) / diag
    return pressure, seg_pressure
```

```python
import functools

import jax
import jax.numpy as jnp
from jax import lax
from jax.experimental import pallas as pl
from jax.experimental.pallas import tpu as pltpu
from jax.sharding import PartitionSpec as P

SWEEPS = 6
MESH = pl.DeviceIdType.MESH
WEST, EAST, SOUTH, NORTH = range(4)
C_W, C_E, C_S, C_N, C_EDGE, C_D, C_U, C_INV, C_RHS = range(9)


def kernel(
    reach,
    rhs_ref,
    acc_ref,
    tx_ref,
    ty_ref,
    tz_ref,
    held_ref,
    host_ref,
    wi_ref,
    sc_ref,
    sr_ref,
    p_out,
    s_out,
    p_buf,
    halo,
    y_stage,
    coef,
    tx_halo,
    ty_halo,
    ty_stage,
    packs,
    params,
    held_buf,
    slot_z,
    seg_buf,
    seg_recv,
    init_send,
    init_recv,
    halo_send,
    halo_recv,
    seg_send,
    seg_rsem,
):
    cx, cy, cz = rhs_ref.shape
    wells = wi_ref.shape[1]
    rows = reach * wells
    gx, gy = lax.axis_index("gx"), lax.axis_index("gy")
    nx, ny = lax.axis_size("gx"), lax.axis_size("gy")
    has_w, has_e = gx > 0, gx < nx - 1
    has_s, has_n = gy > 0, gy < ny - 1
    offsets = [d for d in range(1 - reach, reach) if d != 0]
    index_of = {d: i for i, d in enumerate(offsets)}

    def along_x(d):
        return {"gx": lax.rem(gx + d + nx, nx)}

    def send(src, dst, ssem, rsem, device):
        return pltpu.make_async_remote_copy(
            src_ref=src,
            dst_ref=dst,
            send_sem=ssem,
            recv_sem=rsem,
            device_id=device,
            device_id_type=MESH,
        )

    zero = jnp.zeros((cy, cz), jnp.float32)
    for t in range(SWEEPS):
        for side in range(4):
            halo[t, side] = zero
    tx_halo[...] = zero
    ty_halo[...] = zero

    barrier = pltpu.get_barrier_semaphore()
    for d in offsets:
        pl.semaphore_signal(barrier, inc=1, device_id=along_x(d), device_id_type=MESH)

    @pl.when(has_s)
    def _():
        pl.semaphore_signal(barrier, inc=1, device_id={"gy": gy - 1}, device_id_type=MESH)

    @pl.when(has_n)
    def _():
        pl.semaphore_signal(barrier, inc=1, device_id={"gy": gy + 1}, device_id_type=MESH)

    packs[0, 0:wells] = host_ref[0].astype(jnp.float32)
    packs[0, wells : 2 * wells] = wi_ref[0]
    packs[0, 2 * wells : 3 * wells] = sc_ref[0]
    packs[0, 3 * wells : 4 * wells] = sr_ref[0]
    ty_stage[...] = ty_ref[:, cy - 1, :]
    pl.semaphore_wait(
        barrier, len(offsets) + has_s.astype(jnp.int32) + has_n.astype(jnp.int32)
    )

    def pack_copy(d):
        return send(
            packs.at[0], packs.at[d], init_send.at[d], init_recv.at[d], along_x(d)
        )

    def tx_copy():
        return send(
            tx_ref.at[cx - 1], tx_halo, init_send.at[0], init_recv.at[0], along_x(1)
        )

    def ty_copy():
        return send(
            ty_stage, ty_halo, init_send.at[reach], init_recv.at[reach], {"gy": gy + 1}
        )

    for d in range(reach - 1, 0, -1):
        pack_copy(d).start()
    pl.when(has_e)(lambda: tx_copy().start())
    pl.when(has_n)(lambda: ty_copy().start())

    for r in range(reach):
        held_buf[r * wells : (r + 1) * wells] = held_ref[r, 0]
    held = held_buf[...]
    row_of = held // cz
    z_of = held - row_of * cz
    z_iota = lax.broadcasted_iota(jnp.int32, (cz, cz), 0)
    for s in range(rows):
        hit = (z_iota == jnp.broadcast_to(z_of[s : s + 1, :], (cz, cz))).astype(jnp.float32)
        slot_z[s * cz : (s + 1) * cz, :] = hit.T.astype(jnp.bfloat16)
    row_iota = lax.broadcasted_iota(jnp.int32, (cx * cy, cz), 0)

    lane = lax.broadcasted_iota(jnp.int32, (cy, cz), 1)
    sub = lax.broadcasted_iota(jnp.int32, (cy, cz), 0)
    level = (lax.broadcasted_iota(jnp.int32, (rows, cz), 0) // wells).astype(jnp.float32)

    for d in range(1, reach):
        pack_copy(d).wait_recv()
    for r in range(reach):
        for k in range(4):
            params[k, r * wells : (r + 1) * wells] = packs[r, k * wells : (k + 1) * wells]
    host = params[0]
    wi = params[1]
    rate = params[3]
    slot = lax.broadcasted_iota(jnp.int32, (rows, cz), 1)
    fm = jnp.where(slot > 0, params[2], 0.0)
    fp = jnp.where(slot < cz - 1, pltpu.roll(fm, cz - 1, 1), 0.0)
    seg_inv = 0.8 / (wi + fm + fp)
    mine = host == level

    def gather(t):
        cell_p = jnp.zeros((rows, cz), jnp.float32)
        for x in range(cx):
            for y in range(cy):
                line = jnp.broadcast_to(p_buf[t, x, pl.ds(y, 1), :], (rows, cz))
                got = jnp.take_along_axis(line, z_of, axis=1, mode="promise_in_bounds")
                cell_p = jnp.where(row_of == x * cy + y, got, cell_p)
        return cell_p

    def scatter(flux):
        high = flux.astype(jnp.bfloat16).astype(jnp.float32)
        rest = flux - high
        mid = rest.astype(jnp.bfloat16).astype(jnp.float32)
        low = rest - mid
        parts = []
        for part in (high, mid, low):
            pieces = []
            for s in range(rows):
                at_row = row_iota == jnp.broadcast_to(row_of[s : s + 1, :], row_iota.shape)
                pieces.append(
                    jnp.where(at_row, jnp.broadcast_to(part[s : s + 1, :], row_iota.shape), 0.0)
                )
            parts.append(jnp.concatenate(pieces, axis=1).astype(jnp.bfloat16))
        spread = jnp.dot(
            jnp.concatenate(parts, axis=0), slot_z[...], preferred_element_type=jnp.float32
        )
        cells = cx * cy
        return spread[:cells] + spread[cells : 2 * cells] + spread[2 * cells :]

    def halo_copies(t):
        return (
            (has_w, send(p_buf.at[t, 0], halo.at[t, EAST], halo_send.at[t, WEST],
                         halo_recv.at[t, EAST], {"gx": gx - 1})),
            (has_e, send(p_buf.at[t, cx - 1], halo.at[t, WEST], halo_send.at[t, EAST],
                         halo_recv.at[t, WEST], {"gx": gx + 1})),
            (has_s, send(y_stage.at[t, 0], halo.at[t, NORTH], halo_send.at[t, SOUTH],
                         halo_recv.at[t, NORTH], {"gy": gy - 1})),
            (has_n, send(y_stage.at[t, 1], halo.at[t, SOUTH], halo_send.at[t, NORTH],
                         halo_recv.at[t, SOUTH], {"gy": gy + 1})),
        )

    def send_halos(t):
        y_stage[t, 0] = p_buf[t, :, 0, :]
        y_stage[t, 1] = p_buf[t, :, cy - 1, :]
        for there, copy in halo_copies(t):
            pl.when(there)(copy.start)

    def wait_halos(t):
        for there, slot_at in ((has_w, WEST), (has_e, EAST), (has_s, SOUTH), (has_n, NORTH)):
            copy = send(halo.at[t, slot_at], halo.at[t, slot_at], halo_send.at[t, slot_at],
                        halo_recv.at[t, slot_at], along_x(1))
            pl.when(there)(copy.wait_recv)

    def seg_copy(t, d):
        return send(seg_buf.at[t], seg_recv.at[t, index_of[-d]],
                    seg_send.at[t, index_of[d]], seg_rsem.at[t, index_of[-d]], along_x(d))

    def merge(t, seg):
        for d in offsets:
            seg_copy(t, d).wait_recv()
        for d in offsets:
            got = seg_recv[t, index_of[d]]
            got = pltpu.roll(got, (-d * wells) % rows, 0)
            seg = jnp.where(host == level + d, got, seg)
        return seg

    def well_step(t, seg, cell_p):
        before = pltpu.roll(seg, 1, 1)
        after = pltpu.roll(seg, cz - 1, 1)
        seg = 0.2 * seg + seg_inv * (rate + wi * cell_p + fm * before + fp * after)
        seg_buf[t] = seg
        for d in offsets:
            seg_copy(t, d).start()
        return seg

    def grid_step(t, well_term, result, at):
        parts = []
        for x in range(cx):
            p = p_buf[t, x]
            total = 0.3 * p + coef[C_RHS, x] - coef[C_INV, x] * well_term[x * cy : (x + 1) * cy]
            total += coef[C_U, x] * pltpu.roll(p, cz - 1, 1) + coef[C_D, x] * pltpu.roll(p, 1, 1)
            total += coef[C_N, x] * pltpu.roll(p, cy - 1, 0) + coef[C_S, x] * pltpu.roll(p, 1, 0)
            if x > 0:
                total += coef[C_W, x] * p_buf[t, x - 1]
            if x < cx - 1:
                total += coef[C_E, x] * p_buf[t, x + 1]
            parts.append(total)
        wait_halos(t)
        parts[0] += coef[C_W, 0] * halo[t, WEST]
        parts[-1] += coef[C_E, cx - 1] * halo[t, EAST]
        for x in range(cx):
            north = jnp.broadcast_to(halo[t, NORTH, pl.ds(x, 1), :], (cy, cz))
            south = jnp.broadcast_to(halo[t, SOUTH, pl.ds(x, 1), :], (cy, cz))
            edge = jnp.where(sub == 0, south, north)
            value = parts[x] + coef[C_EDGE, x] * edge
            if at is None:
                result[x] = value
            else:
                result[at, x] = value

    seg = seg_inv * rate
    well_term = scatter(jnp.where(mine, -wi * seg, 0.0))

    pl.when(has_w)(tx_copy().wait_recv)
    pl.when(has_s)(ty_copy().wait_recv)
    for x in range(cx):
        ex, ey, ez = tx_ref[x], ty_ref[x], tz_ref[x]
        wx = tx_halo[...] if x == 0 else tx_ref[x - 1]
        edge_y = jnp.broadcast_to(ty_halo[pl.ds(x, 1), :], (cy, cz))
        wy = jnp.where(sub == 0, edge_y, pltpu.roll(ey, 1, 0))
        wz = jnp.where(lane == 0, 0.0, pltpu.roll(ez, 1, 1))
        diag = acc_ref[x] + ex + wx + ey + wy + ez + wz
        inv = 0.7 / diag
        coef[C_W, x] = inv * wx
        coef[C_E, x] = inv * ex
        coef[C_S, x] = jnp.where(sub == 0, 0.0, inv * wy)
        coef[C_N, x] = jnp.where(sub == cy - 1, 0.0, inv * ey)
        coef[C_EDGE, x] = jnp.where(
            sub == 0, inv * wy, jnp.where(sub == cy - 1, inv * ey, 0.0)
        )
        coef[C_D, x] = inv * wz
        coef[C_U, x] = jnp.where(lane == cz - 1, 0.0, inv * ez)
        coef[C_INV, x] = inv
        right = inv * rhs_ref[x]
        coef[C_RHS, x] = right
        p_buf[1, x] = right - inv * well_term[x * cy : (x + 1) * cy]
    send_halos(1)

    def sweep(t, seg, first):
        cell_p = gather(t)
        if not first:
            seg = merge(t - 1, seg)
        seg = well_step(t, seg, cell_p)
        well_term = scatter(jnp.where(mine, wi * (cell_p - seg), 0.0))
        return seg, well_term

    def middle(t, seg, first):
        seg, well_term = sweep(t, seg, first)
        grid_step(t, well_term, p_buf, t + 1)
        send_halos(t + 1)
        return seg

    seg = middle(1, seg, True)
    seg = lax.fori_loop(2, SWEEPS - 1, lambda t, seg: middle(t, seg, False), seg)
    last = SWEEPS - 1
    seg, well_term = sweep(last, seg, False)
    grid_step(last, well_term, p_out, None)
    seg = merge(last, seg)
    s_out[0] = seg[:wells]

    for d in range(1, reach):
        pack_copy(d).wait_send()
    pl.when(has_e)(lambda: tx_copy().wait_send())
    pl.when(has_n)(lambda: ty_copy().wait_send())

    def drain(t, carry):
        for there, copy in halo_copies(t):
            pl.when(there)(copy.wait_send)
        for d in offsets:
            seg_copy(t, d).wait_send()
        return carry

    lax.fori_loop(1, SWEEPS, drain, 0)


def shards(rhs, acc, tx, ty, tz, held, host, wi, sc, sr):
    reach = held.shape[0]
    wells, slots = wi.shape[1:]
    rows = reach * wells
    cx, cy, cz = rhs.shape
    peers = 2 * (reach - 1)
    vmem = pl.BlockSpec(memory_space=pltpu.VMEM)
    f32 = jnp.float32
    return pl.pallas_call(
        functools.partial(kernel, reach),
        out_shape=(
            jax.ShapeDtypeStruct(rhs.shape, f32),
            jax.ShapeDtypeStruct(sr.shape, f32),
        ),
        in_specs=[vmem] * 10,
        out_specs=(vmem, vmem),
        scratch_shapes=[
            pltpu.VMEM((SWEEPS, cx, cy, cz), f32),
            pltpu.VMEM((SWEEPS, 4, cy, cz), f32),
            pltpu.VMEM((SWEEPS, 2, cx, cz), f32),
            pltpu.VMEM((9, cx, cy, cz), f32),
            pltpu.VMEM((cy, cz), f32),
            pltpu.VMEM((cx, cz), f32),
            pltpu.VMEM((cx, cz), f32),
            pltpu.VMEM((reach, 4 * wells, slots), f32),
            pltpu.VMEM((4, rows, slots), f32),
            pltpu.VMEM((rows, slots), jnp.int32),
            pltpu.VMEM((rows * slots, cz), jnp.bfloat16),
            pltpu.VMEM((SWEEPS, rows, slots), f32),
            pltpu.VMEM((SWEEPS, peers, rows, slots), f32),
            pltpu.SemaphoreType.DMA((reach + 1,)),
            pltpu.SemaphoreType.DMA((reach + 1,)),
            pltpu.SemaphoreType.DMA((SWEEPS, 4)),
            pltpu.SemaphoreType.DMA((SWEEPS, 4)),
            pltpu.SemaphoreType.DMA((SWEEPS, peers)),
            pltpu.SemaphoreType.DMA((SWEEPS, peers)),
        ],
        compiler_params=pltpu.CompilerParams(
            collective_id=0, has_side_effects=True, vmem_limit_bytes=32 * 1024 * 1024
        ),
    )(rhs, acc, tx, ty, tz, held, host, wi, sc, sr)


def solution(mesh):
    return jax.shard_map(
        shards,
        mesh=mesh,
        in_specs=(P("gx", "gy", None),) * 5
        + (P(None, "gx", "gy", None),)
        + (P("gx", "gy", None),) * 4,
        out_specs=(P("gx", "gy", None), P("gx", "gy", None)),
        check_vma=False,
    )
```

```python
import functools

import jax
import jax.numpy as jnp
from jax import lax
from jax.experimental import pallas as pl
from jax.experimental.pallas import tpu as pltpu
from jax.sharding import PartitionSpec as P

SWEEPS = 6
MESH = pl.DeviceIdType.MESH
WEST, EAST, SOUTH, NORTH = range(4)
C_W, C_E, C_S, C_N, C_EDGE, C_D, C_U, C_INV, C_RHS = range(9)


def kernel(
    reach,
    rhs_hbm,
    acc_hbm,
    tx_hbm,
    ty_hbm,
    tz_hbm,
    held_hbm,
    host_hbm,
    wi_hbm,
    sc_hbm,
    sr_hbm,
    p_out,
    s_out,
    rhs_ref,
    acc_ref,
    tx_ref,
    ty_ref,
    tz_ref,
    held_ref,
    host_ref,
    wi_ref,
    sc_ref,
    sr_ref,
    fetch_sem,
    p_buf,
    halo,
    y_stage,
    coef,
    tx_halo,
    ty_halo,
    ty_stage,
    packs,
    params,
    held_buf,
    slot_z,
    cell_buf,
    cell_recv,
    init_send,
    init_recv,
    halo_send,
    halo_recv,
    cell_send,
    cell_rsem,
):
    cx, cy, cz = rhs_ref.shape
    wells = wi_ref.shape[1]
    rows = reach * wells
    gx, gy = lax.axis_index("gx"), lax.axis_index("gy")
    nx, ny = lax.axis_size("gx"), lax.axis_size("gy")
    has_w, has_e = gx > 0, gx < nx - 1
    has_s, has_n = gy > 0, gy < ny - 1
    offsets = [d for d in range(1 - reach, reach) if d != 0]
    index_of = {d: i for i, d in enumerate(offsets)}

    def along_x(d):
        return {"gx": lax.rem(gx + d + nx, nx)}

    def send(src, dst, ssem, rsem, device):
        return pltpu.make_async_remote_copy(
            src_ref=src,
            dst_ref=dst,
            send_sem=ssem,
            recv_sem=rsem,
            device_id=device,
            device_id_type=MESH,
        )

    zero = jnp.zeros((cy, cz), jnp.float32)
    for t in range(SWEEPS):
        for side in range(4):
            halo[t, side] = zero
    tx_halo[...] = zero
    ty_halo[...] = zero

    barrier = pltpu.get_barrier_semaphore()
    for d in offsets:
        pl.semaphore_signal(barrier, inc=1, device_id=along_x(d), device_id_type=MESH)

    @pl.when(has_s)
    def _():
        pl.semaphore_signal(barrier, inc=1, device_id={"gy": gy - 1}, device_id_type=MESH)

    @pl.when(has_n)
    def _():
        pl.semaphore_signal(barrier, inc=1, device_id={"gy": gy + 1}, device_id_type=MESH)

    fetches = [
        pltpu.make_async_copy(src, dst, fetch_sem.at[i])
        for i, (src, dst) in enumerate(
            (
                (host_hbm, host_ref),
                (wi_hbm, wi_ref),
                (sc_hbm, sc_ref),
                (sr_hbm, sr_ref),
                (ty_hbm, ty_ref),
                (tx_hbm, tx_ref),
                (held_hbm, held_ref),
                (acc_hbm, acc_ref),
                (tz_hbm, tz_ref),
                (rhs_hbm, rhs_ref),
            )
        )
    ]
    for fetch in fetches:
        fetch.start()
    for fetch in fetches[:6]:
        fetch.wait()
    packs[0, 0:wells] = host_ref[0].astype(jnp.float32)
    packs[0, wells : 2 * wells] = wi_ref[0]
    packs[0, 2 * wells : 3 * wells] = sc_ref[0]
    packs[0, 3 * wells : 4 * wells] = sr_ref[0]
    ty_stage[...] = ty_ref[:, cy - 1, :]
    pl.semaphore_wait(
        barrier, len(offsets) + has_s.astype(jnp.int32) + has_n.astype(jnp.int32)
    )

    def pack_copy(d):
        return send(
            packs.at[0], packs.at[d], init_send.at[d], init_recv.at[d], along_x(d)
        )

    def tx_copy():
        return send(
            tx_ref.at[cx - 1], tx_halo, init_send.at[0], init_recv.at[0], along_x(1)
        )

    def ty_copy():
        return send(
            ty_stage, ty_halo, init_send.at[reach], init_recv.at[reach], {"gy": gy + 1}
        )

    for d in range(reach - 1, 0, -1):
        pack_copy(d).start()
    pl.when(has_e)(lambda: tx_copy().start())
    pl.when(has_n)(lambda: ty_copy().start())

    for fetch in fetches[6:]:
        fetch.wait()

    for r in range(reach):
        held_buf[r * wells : (r + 1) * wells] = held_ref[r, 0]
    held = held_buf[...]
    row_of = held // cz
    z_of = held - row_of * cz
    z_iota = lax.broadcasted_iota(jnp.int32, (cz, cz), 0)
    for s in range(rows):
        hit = (z_iota == jnp.broadcast_to(z_of[s : s + 1, :], (cz, cz))).astype(jnp.float32)
        slot_z[s * cz : (s + 1) * cz, :] = hit.T.astype(jnp.bfloat16)
    row_iota = lax.broadcasted_iota(jnp.int32, (cx * cy, cz), 0)

    lane = lax.broadcasted_iota(jnp.int32, (cy, cz), 1)
    sub = lax.broadcasted_iota(jnp.int32, (cy, cz), 0)
    level = (lax.broadcasted_iota(jnp.int32, (rows, cz), 0) // wells).astype(jnp.float32)

    def gather(t):
        found = []
        for x in range(cx):
            cell_p = jnp.zeros((rows, cz), jnp.float32)
            for y in range(cy):
                line = jnp.broadcast_to(p_buf[t, x, pl.ds(y, 1), :], (rows, cz))
                got = jnp.take_along_axis(line, z_of, axis=1, mode="promise_in_bounds")
                cell_p = jnp.where(row_of == x * cy + y, got, cell_p)
            found.append(cell_p)
        while len(found) > 1:
            found = [sum(found[i : i + 2]) for i in range(0, len(found), 2)]
        return found[0]

    def scatter(flux):
        high = flux.astype(jnp.bfloat16).astype(jnp.float32)
        rest = flux - high
        mid = rest.astype(jnp.bfloat16).astype(jnp.float32)
        low = rest - mid
        parts = []
        for part in (high, mid, low):
            pieces = []
            for s in range(rows):
                at_row = row_iota == jnp.broadcast_to(row_of[s : s + 1, :], row_iota.shape)
                pieces.append(
                    jnp.where(at_row, jnp.broadcast_to(part[s : s + 1, :], row_iota.shape), 0.0)
                )
            parts.append(jnp.concatenate(pieces, axis=1).astype(jnp.bfloat16))
        spread = jnp.dot(
            jnp.concatenate(parts, axis=0), slot_z[...], preferred_element_type=jnp.float32
        )
        cells = cx * cy
        return spread[:cells] + spread[cells : 2 * cells] + spread[2 * cells :]

    def halo_copies(t):
        return (
            (has_w, send(p_buf.at[t, 0], halo.at[t, EAST], halo_send.at[t, WEST],
                         halo_recv.at[t, EAST], {"gx": gx - 1})),
            (has_e, send(p_buf.at[t, cx - 1], halo.at[t, WEST], halo_send.at[t, EAST],
                         halo_recv.at[t, WEST], {"gx": gx + 1})),
            (has_s, send(y_stage.at[t, 0], halo.at[t, NORTH], halo_send.at[t, SOUTH],
                         halo_recv.at[t, NORTH], {"gy": gy - 1})),
            (has_n, send(y_stage.at[t, 1], halo.at[t, SOUTH], halo_send.at[t, NORTH],
                         halo_recv.at[t, SOUTH], {"gy": gy + 1})),
        )

    def send_halos(t):
        y_stage[t, 0] = p_buf[t, :, 0, :]
        y_stage[t, 1] = p_buf[t, :, cy - 1, :]
        for there, copy in halo_copies(t):
            pl.when(there)(copy.start)

    def wait_halos(t):
        for there, slot_at in ((has_w, WEST), (has_e, EAST), (has_s, SOUTH), (has_n, NORTH)):
            copy = send(halo.at[t, slot_at], halo.at[t, slot_at], halo_send.at[t, slot_at],
                        halo_recv.at[t, slot_at], along_x(1))
            pl.when(there)(copy.wait_recv)

    def cell_copy(t, d):
        return send(cell_buf.at[t], cell_recv.at[t, index_of[-d]],
                    cell_send.at[t, index_of[d]], cell_rsem.at[t, index_of[-d]], along_x(d))

    def merge(t):
        cell_p = cell_buf[t]
        for d in offsets:
            cell_copy(t, d).wait_recv()
        for d in offsets:
            got = pltpu.roll(cell_recv[t, index_of[d]], (-d * wells) % rows, 0)
            cell_p = jnp.where(host == level + d, got, cell_p)
        return cell_p

    def well_step(seg, cell_p):
        before = pltpu.roll(seg, 1, 1)
        after = pltpu.roll(seg, cz - 1, 1)
        return 0.2 * seg + seg_inv * (rate + wi * cell_p + fm * before + fp * after)

    def grid_step(t, well_term, result, at):
        parts = []
        for x in range(cx):
            p = p_buf[t, x]
            total = 0.3 * p + coef[C_RHS, x] - coef[C_INV, x] * well_term[x * cy : (x + 1) * cy]
            total += coef[C_U, x] * pltpu.roll(p, cz - 1, 1) + coef[C_D, x] * pltpu.roll(p, 1, 1)
            total += coef[C_N, x] * pltpu.roll(p, cy - 1, 0) + coef[C_S, x] * pltpu.roll(p, 1, 0)
            if x > 0:
                total += coef[C_W, x] * p_buf[t, x - 1]
            if x < cx - 1:
                total += coef[C_E, x] * p_buf[t, x + 1]
            parts.append(total)
        wait_halos(t)
        parts[0] += coef[C_W, 0] * halo[t, WEST]
        parts[-1] += coef[C_E, cx - 1] * halo[t, EAST]
        for x in range(cx):
            north = jnp.broadcast_to(halo[t, NORTH, pl.ds(x, 1), :], (cy, cz))
            south = jnp.broadcast_to(halo[t, SOUTH, pl.ds(x, 1), :], (cy, cz))
            edge = jnp.where(sub == 0, south, north)
            value = parts[x] + coef[C_EDGE, x] * edge
            if at is None:
                result[x] = value
            else:
                result[at, x] = value

    pl.when(has_w)(tx_copy().wait_recv)
    pl.when(has_s)(ty_copy().wait_recv)
    for x in range(cx):
        ex, ey, ez = tx_ref[x], ty_ref[x], tz_ref[x]
        wx = tx_halo[...] if x == 0 else tx_ref[x - 1]
        edge_y = jnp.broadcast_to(ty_halo[pl.ds(x, 1), :], (cy, cz))
        wy = jnp.where(sub == 0, edge_y, pltpu.roll(ey, 1, 0))
        wz = jnp.where(lane == 0, 0.0, pltpu.roll(ez, 1, 1))
        diag = acc_ref[x] + ex + wx + ey + wy + ez + wz
        inv = 0.7 / diag
        coef[C_W, x] = inv * wx
        coef[C_E, x] = inv * ex
        coef[C_S, x] = jnp.where(sub == 0, 0.0, inv * wy)
        coef[C_N, x] = jnp.where(sub == cy - 1, 0.0, inv * ey)
        coef[C_EDGE, x] = jnp.where(
            sub == 0, inv * wy, jnp.where(sub == cy - 1, inv * ey, 0.0)
        )
        coef[C_D, x] = inv * wz
        coef[C_U, x] = jnp.where(lane == cz - 1, 0.0, inv * ez)
        coef[C_INV, x] = inv
        coef[C_RHS, x] = inv * rhs_ref[x]

    for d in range(1, reach):
        pack_copy(d).wait_recv()
    for r in range(reach):
        for k in range(4):
            params[k, r * wells : (r + 1) * wells] = packs[r, k * wells : (k + 1) * wells]
    host = params[0]
    wi = params[1]
    rate = params[3]
    slot = lax.broadcasted_iota(jnp.int32, (rows, cz), 1)
    fm = jnp.where(slot > 0, params[2], 0.0)
    fp = jnp.where(slot < cz - 1, pltpu.roll(fm, cz - 1, 1), 0.0)
    seg_inv = 0.8 / (wi + fm + fp)
    mine = host == level

    seg = seg_inv * rate
    well_term = scatter(jnp.where(mine, -wi * seg, 0.0))
    for x in range(cx):
        p_buf[1, x] = coef[C_RHS, x] - coef[C_INV, x] * well_term[x * cy : (x + 1) * cy]
    send_halos(1)

    def sweep(t, seg, first):
        cell_p = gather(t)
        cell_buf[t] = cell_p
        for d in offsets:
            cell_copy(t, d).start()
        if not first:
            seg = well_step(seg, merge(t - 1))
        flux = wi * (cell_p - well_step(seg, cell_p))
        well_term = scatter(jnp.where(mine, flux, 0.0))
        return seg, well_term

    def middle(t, seg, first):
        seg, well_term = sweep(t, seg, first)
        grid_step(t, well_term, p_buf, t + 1)
        send_halos(t + 1)
        return seg

    seg = middle(1, seg, True)
    seg = lax.fori_loop(2, SWEEPS - 1, lambda t, seg: middle(t, seg, False), seg)
    last = SWEEPS - 1
    seg, well_term = sweep(last, seg, False)
    grid_step(last, well_term, p_out, None)
    seg = well_step(seg, merge(last))
    s_out[0] = seg[:wells]

    for d in range(1, reach):
        pack_copy(d).wait_send()
    pl.when(has_e)(lambda: tx_copy().wait_send())
    pl.when(has_n)(lambda: ty_copy().wait_send())

    def drain(t, carry):
        for there, copy in halo_copies(t):
            pl.when(there)(copy.wait_send)
        for d in offsets:
            cell_copy(t, d).wait_send()
        return carry

    lax.fori_loop(1, SWEEPS, drain, 0)


def shards(*args):
    rhs, acc, tx, ty, tz, held, host, wi, sc, sr = args
    reach = held.shape[0]
    wells, slots = wi.shape[1:]
    rows = reach * wells
    cx, cy, cz = rhs.shape
    peers = 2 * (reach - 1)
    vmem = pl.BlockSpec(memory_space=pltpu.VMEM)
    f32 = jnp.float32
    return pl.pallas_call(
        functools.partial(kernel, reach),
        out_shape=(
            jax.ShapeDtypeStruct(rhs.shape, f32),
            jax.ShapeDtypeStruct(sr.shape, f32),
        ),
        in_specs=[pl.BlockSpec(memory_space=pltpu.HBM)] * 10,
        out_specs=(vmem, vmem),
        scratch_shapes=[pltpu.VMEM(a.shape, a.dtype) for a in args]
        + [
            pltpu.SemaphoreType.DMA((len(args),)),
            pltpu.VMEM((SWEEPS, cx, cy, cz), f32),
            pltpu.VMEM((SWEEPS, 4, cy, cz), f32),
            pltpu.VMEM((SWEEPS, 2, cx, cz), f32),
            pltpu.VMEM((9, cx, cy, cz), f32),
            pltpu.VMEM((cy, cz), f32),
            pltpu.VMEM((cx, cz), f32),
            pltpu.VMEM((cx, cz), f32),
            pltpu.VMEM((reach, 4 * wells, slots), f32),
            pltpu.VMEM((4, rows, slots), f32),
            pltpu.VMEM((rows, slots), jnp.int32),
            pltpu.VMEM((rows * slots, cz), jnp.bfloat16),
            pltpu.VMEM((SWEEPS, rows, slots), f32),
            pltpu.VMEM((SWEEPS, peers, rows, slots), f32),
            pltpu.SemaphoreType.DMA((reach + 1,)),
            pltpu.SemaphoreType.DMA((reach + 1,)),
            pltpu.SemaphoreType.DMA((SWEEPS, 4)),
            pltpu.SemaphoreType.DMA((SWEEPS, 4)),
            pltpu.SemaphoreType.DMA((SWEEPS, peers)),
            pltpu.SemaphoreType.DMA((SWEEPS, peers)),
        ],
        compiler_params=pltpu.CompilerParams(
            collective_id=0, has_side_effects=True, vmem_limit_bytes=60 * 1024 * 1024
        ),
    )(*args)


def solution(mesh):
    return jax.shard_map(
        shards,
        mesh=mesh,
        in_specs=(P("gx", "gy", None),) * 5
        + (P(None, "gx", "gy", None),)
        + (P("gx", "gy", None),) * 4,
        out_specs=(P("gx", "gy", None), P("gx", "gy", None)),
        check_vma=False,
    )
```

```python
import functools

import jax
import jax.numpy as jnp
from jax import lax
from jax.experimental import pallas as pl
from jax.experimental.pallas import tpu as pltpu
from jax.sharding import PartitionSpec as P

SWEEPS = 6
MESH = pl.DeviceIdType.MESH
WEST, EAST, SOUTH, NORTH = range(4)
C_W, C_E, C_S, C_N, C_EDGE, C_D, C_U, C_INV, C_RHS = range(9)


def kernel(
    reach,
    rhs_hbm,
    acc_hbm,
    tx_hbm,
    ty_hbm,
    tz_hbm,
    held_hbm,
    host_hbm,
    wi_hbm,
    sc_hbm,
    sr_hbm,
    p_out,
    s_out,
    rhs_ref,
    acc_ref,
    tx_ref,
    ty_ref,
    tz_ref,
    held_ref,
    host_ref,
    wi_ref,
    sc_ref,
    sr_ref,
    fetch_sem,
    p_buf,
    halo,
    y_stage,
    coef,
    tx_halo,
    ty_halo,
    ty_stage,
    packs,
    params,
    held_buf,
    slot_column,
    cell_buf,
    cell_recv,
    init_send,
    init_recv,
    halo_send,
    halo_recv,
    cell_send,
    cell_rsem,
):
    cx, cy, cz = rhs_ref.shape
    wells = wi_ref.shape[1]
    rows = reach * wells
    gx, gy = lax.axis_index("gx"), lax.axis_index("gy")
    nx, ny = lax.axis_size("gx"), lax.axis_size("gy")
    has_w, has_e = gx > 0, gx < nx - 1
    has_s, has_n = gy > 0, gy < ny - 1
    offsets = [d for d in range(1 - reach, reach) if d != 0]
    index_of = {d: i for i, d in enumerate(offsets)}

    def along_x(d):
        return {"gx": lax.rem(gx + d + nx, nx)}

    def send(src, dst, ssem, rsem, device):
        return pltpu.make_async_remote_copy(
            src_ref=src,
            dst_ref=dst,
            send_sem=ssem,
            recv_sem=rsem,
            device_id=device,
            device_id_type=MESH,
        )

    zero = jnp.zeros((cy, cz), jnp.float32)
    for t in range(SWEEPS):
        for side in range(4):
            halo[t, side] = zero
    tx_halo[...] = zero
    ty_halo[...] = zero

    barrier = pltpu.get_barrier_semaphore()
    for d in offsets:
        pl.semaphore_signal(barrier, inc=1, device_id=along_x(d), device_id_type=MESH)

    @pl.when(has_s)
    def _():
        pl.semaphore_signal(barrier, inc=1, device_id={"gy": gy - 1}, device_id_type=MESH)

    @pl.when(has_n)
    def _():
        pl.semaphore_signal(barrier, inc=1, device_id={"gy": gy + 1}, device_id_type=MESH)

    fetches = [
        pltpu.make_async_copy(src, dst, fetch_sem.at[i])
        for i, (src, dst) in enumerate(
            (
                (host_hbm, host_ref),
                (wi_hbm, wi_ref),
                (sc_hbm, sc_ref),
                (sr_hbm, sr_ref),
                (ty_hbm, ty_ref),
                (tx_hbm, tx_ref),
                (held_hbm, held_ref),
                (acc_hbm, acc_ref),
                (tz_hbm, tz_ref),
                (rhs_hbm, rhs_ref),
            )
        )
    ]
    for fetch in fetches:
        fetch.start()
    for fetch in fetches[:6]:
        fetch.wait()
    packs[0, 0:wells] = host_ref[0].astype(jnp.float32)
    packs[0, wells : 2 * wells] = wi_ref[0]
    packs[0, 2 * wells : 3 * wells] = sc_ref[0]
    packs[0, 3 * wells : 4 * wells] = sr_ref[0]
    ty_stage[...] = ty_ref[:, cy - 1, :]
    pl.semaphore_wait(
        barrier, len(offsets) + has_s.astype(jnp.int32) + has_n.astype(jnp.int32)
    )

    def pack_copy(d):
        return send(
            packs.at[0], packs.at[d], init_send.at[d], init_recv.at[d], along_x(d)
        )

    def tx_copy():
        return send(
            tx_ref.at[cx - 1], tx_halo, init_send.at[0], init_recv.at[0], along_x(1)
        )

    def ty_copy():
        return send(
            ty_stage, ty_halo, init_send.at[reach], init_recv.at[reach], {"gy": gy + 1}
        )

    for d in range(reach - 1, 0, -1):
        pack_copy(d).start()
    pl.when(has_e)(lambda: tx_copy().start())
    pl.when(has_n)(lambda: ty_copy().start())

    for fetch in fetches[6:]:
        fetch.wait()

    for r in range(reach):
        held_buf[r * wells : (r + 1) * wells] = held_ref[r, 0]
    held = held_buf[...]
    row_of = held // cz
    z_of = held - row_of * cz
    lines = cx * cy // 2
    half_of = row_of // lines
    line_of = row_of - half_of * lines
    column_of = half_of * cz + z_of
    column_iota = lax.broadcasted_iota(jnp.int32, (2 * cz, cz), 0)
    for s in range(rows):
        column = jnp.broadcast_to(column_of[s : s + 1, :], column_iota.shape)
        hit = (column_iota == column).astype(jnp.float32)
        slot_column[s * cz : (s + 1) * cz, :] = hit.T.astype(jnp.bfloat16)
    line_iota = lax.broadcasted_iota(jnp.int32, (lines, cz), 0)

    lane = lax.broadcasted_iota(jnp.int32, (cy, cz), 1)
    sub = lax.broadcasted_iota(jnp.int32, (cy, cz), 0)
    level = (lax.broadcasted_iota(jnp.int32, (rows, cz), 0) // wells).astype(jnp.float32)

    def gather(t):
        found = []
        for x in range(cx):
            cell_p = jnp.zeros((rows, cz), jnp.float32)
            for y in range(cy):
                line = jnp.broadcast_to(p_buf[t, x, pl.ds(y, 1), :], (rows, cz))
                got = jnp.take_along_axis(line, z_of, axis=1, mode="promise_in_bounds")
                cell_p = jnp.where(row_of == x * cy + y, got, cell_p)
            found.append(cell_p)
        while len(found) > 1:
            found = [sum(found[i : i + 2]) for i in range(0, len(found), 2)]
        return found[0]

    def scatter(flux):
        high = flux.astype(jnp.bfloat16).astype(jnp.float32)
        rest = flux - high
        mid = rest.astype(jnp.bfloat16).astype(jnp.float32)
        low = rest - mid
        pieces = []
        for s in range(rows):
            at_line = line_iota == jnp.broadcast_to(line_of[s : s + 1, :], line_iota.shape)
            pieces.append(
                jnp.concatenate(
                    [
                        jnp.where(at_line, jnp.broadcast_to(part[s : s + 1, :], at_line.shape), 0.0)
                        for part in (high, mid, low)
                    ],
                    axis=0,
                ).astype(jnp.bfloat16)
            )
        spread = jnp.dot(
            jnp.concatenate(pieces, axis=1), slot_column[...], preferred_element_type=jnp.float32
        )
        spread = spread[:lines] + spread[lines : 2 * lines] + spread[2 * lines :]
        return [
            spread[x % (cx // 2) * cy :][:cy, x // (cx // 2) * cz :][:, :cz] for x in range(cx)
        ]

    def halo_copies(t):
        return (
            (has_w, send(p_buf.at[t, 0], halo.at[t, EAST], halo_send.at[t, WEST],
                         halo_recv.at[t, EAST], {"gx": gx - 1})),
            (has_e, send(p_buf.at[t, cx - 1], halo.at[t, WEST], halo_send.at[t, EAST],
                         halo_recv.at[t, WEST], {"gx": gx + 1})),
            (has_s, send(y_stage.at[t, 0], halo.at[t, NORTH], halo_send.at[t, SOUTH],
                         halo_recv.at[t, NORTH], {"gy": gy - 1})),
            (has_n, send(y_stage.at[t, 1], halo.at[t, SOUTH], halo_send.at[t, NORTH],
                         halo_recv.at[t, SOUTH], {"gy": gy + 1})),
        )

    def send_x(t):
        for there, copy in halo_copies(t)[:2]:
            pl.when(there)(copy.start)

    def send_y(t):
        y_stage[t, 0] = p_buf[t, :, 0, :]
        y_stage[t, 1] = p_buf[t, :, cy - 1, :]
        for there, copy in halo_copies(t)[2:]:
            pl.when(there)(copy.start)

    def wait_halos(t):
        for there, slot_at in ((has_w, WEST), (has_e, EAST), (has_s, SOUTH), (has_n, NORTH)):
            copy = send(halo.at[t, slot_at], halo.at[t, slot_at], halo_send.at[t, slot_at],
                        halo_recv.at[t, slot_at], along_x(1))
            pl.when(there)(copy.wait_recv)

    def cell_copy(t, d):
        return send(cell_buf.at[t], cell_recv.at[t, index_of[-d]],
                    cell_send.at[t, index_of[d]], cell_rsem.at[t, index_of[-d]], along_x(d))

    def merge(t):
        cell_p = cell_buf[t]
        for d in offsets:
            cell_copy(t, d).wait_recv()
        for d in offsets:
            got = pltpu.roll(cell_recv[t, index_of[d]], (-d * wells) % rows, 0)
            cell_p = jnp.where(host == level + d, got, cell_p)
        return cell_p

    def well_step(seg, cell_p):
        before = pltpu.roll(seg, 1, 1)
        after = pltpu.roll(seg, cz - 1, 1)
        return 0.2 * seg + seg_inv * (rate + wi * cell_p + fm * before + fp * after)

    def grid_step(t, well_term, result, at):
        parts = []
        for x in range(cx):
            p = p_buf[t, x]
            total = 0.3 * p + coef[C_RHS, x] - coef[C_INV, x] * well_term[x]
            total += coef[C_U, x] * pltpu.roll(p, cz - 1, 1) + coef[C_D, x] * pltpu.roll(p, 1, 1)
            total += coef[C_N, x] * pltpu.roll(p, cy - 1, 0) + coef[C_S, x] * pltpu.roll(p, 1, 0)
            if x > 0:
                total += coef[C_W, x] * p_buf[t, x - 1]
            if x < cx - 1:
                total += coef[C_E, x] * p_buf[t, x + 1]
            parts.append(total)
        wait_halos(t)
        parts[0] += coef[C_W, 0] * halo[t, WEST]
        parts[-1] += coef[C_E, cx - 1] * halo[t, EAST]
        for place, x in enumerate([0, cx - 1] + list(range(1, cx - 1))):
            north = jnp.broadcast_to(halo[t, NORTH, pl.ds(x, 1), :], (cy, cz))
            south = jnp.broadcast_to(halo[t, SOUTH, pl.ds(x, 1), :], (cy, cz))
            edge = jnp.where(sub == 0, south, north)
            value = parts[x] + coef[C_EDGE, x] * edge
            if at is None:
                result[x] = value
            else:
                result[at, x] = value
                if place == 1:
                    send_x(at)
        if at is not None:
            send_y(at)

    pl.when(has_w)(tx_copy().wait_recv)
    pl.when(has_s)(ty_copy().wait_recv)
    for x in range(cx):
        ex, ey, ez = tx_ref[x], ty_ref[x], tz_ref[x]
        wx = tx_halo[...] if x == 0 else tx_ref[x - 1]
        edge_y = jnp.broadcast_to(ty_halo[pl.ds(x, 1), :], (cy, cz))
        wy = jnp.where(sub == 0, edge_y, pltpu.roll(ey, 1, 0))
        wz = jnp.where(lane == 0, 0.0, pltpu.roll(ez, 1, 1))
        diag = acc_ref[x] + ex + wx + ey + wy + ez + wz
        inv = 0.7 / diag
        coef[C_W, x] = inv * wx
        coef[C_E, x] = inv * ex
        coef[C_S, x] = jnp.where(sub == 0, 0.0, inv * wy)
        coef[C_N, x] = jnp.where(sub == cy - 1, 0.0, inv * ey)
        coef[C_EDGE, x] = jnp.where(
            sub == 0, inv * wy, jnp.where(sub == cy - 1, inv * ey, 0.0)
        )
        coef[C_D, x] = inv * wz
        coef[C_U, x] = jnp.where(lane == cz - 1, 0.0, inv * ez)
        coef[C_INV, x] = inv
        coef[C_RHS, x] = inv * rhs_ref[x]

    for d in range(1, reach):
        pack_copy(d).wait_recv()
    for r in range(reach):
        for k in range(4):
            params[k, r * wells : (r + 1) * wells] = packs[r, k * wells : (k + 1) * wells]
    host = params[0]
    wi = params[1]
    rate = params[3]
    slot = lax.broadcasted_iota(jnp.int32, (rows, cz), 1)
    fm = jnp.where(slot > 0, params[2], 0.0)
    fp = jnp.where(slot < cz - 1, pltpu.roll(fm, cz - 1, 1), 0.0)
    seg_inv = 0.8 / (wi + fm + fp)
    mine = host == level

    seg = seg_inv * rate
    well_term = scatter(jnp.where(mine, -wi * seg, 0.0))
    for x in range(cx):
        p_buf[1, x] = coef[C_RHS, x] - coef[C_INV, x] * well_term[x]
    send_x(1)
    send_y(1)

    def sweep(t, seg, first):
        cell_p = gather(t)
        cell_buf[t] = cell_p
        for d in offsets:
            cell_copy(t, d).start()
        if not first:
            seg = well_step(seg, merge(t - 1))
        flux = wi * (cell_p - well_step(seg, cell_p))
        well_term = scatter(jnp.where(mine, flux, 0.0))
        return seg, well_term

    def middle(t, seg, first):
        seg, well_term = sweep(t, seg, first)
        grid_step(t, well_term, p_buf, t + 1)
        return seg

    seg = middle(1, seg, True)
    seg = lax.fori_loop(2, SWEEPS - 1, lambda t, seg: middle(t, seg, False), seg)
    last = SWEEPS - 1
    seg, well_term = sweep(last, seg, False)
    grid_step(last, well_term, p_out, None)
    seg = well_step(seg, merge(last))
    s_out[0] = seg[:wells]

    for d in range(1, reach):
        pack_copy(d).wait_send()
    pl.when(has_e)(lambda: tx_copy().wait_send())
    pl.when(has_n)(lambda: ty_copy().wait_send())

    def drain(t, carry):
        for there, copy in halo_copies(t):
            pl.when(there)(copy.wait_send)
        for d in offsets:
            cell_copy(t, d).wait_send()
        return carry

    lax.fori_loop(1, SWEEPS, drain, 0)


def shards(*args):
    rhs, acc, tx, ty, tz, held, host, wi, sc, sr = args
    reach = held.shape[0]
    wells, slots = wi.shape[1:]
    rows = reach * wells
    cx, cy, cz = rhs.shape
    peers = 2 * (reach - 1)
    vmem = pl.BlockSpec(memory_space=pltpu.VMEM)
    f32 = jnp.float32
    return pl.pallas_call(
        functools.partial(kernel, reach),
        out_shape=(
            jax.ShapeDtypeStruct(rhs.shape, f32),
            jax.ShapeDtypeStruct(sr.shape, f32),
        ),
        in_specs=[pl.BlockSpec(memory_space=pltpu.HBM)] * 10,
        out_specs=(vmem, vmem),
        scratch_shapes=[pltpu.VMEM(a.shape, a.dtype) for a in args]
        + [
            pltpu.SemaphoreType.DMA((len(args),)),
            pltpu.VMEM((SWEEPS, cx, cy, cz), f32),
            pltpu.VMEM((SWEEPS, 4, cy, cz), f32),
            pltpu.VMEM((SWEEPS, 2, cx, cz), f32),
            pltpu.VMEM((9, cx, cy, cz), f32),
            pltpu.VMEM((cy, cz), f32),
            pltpu.VMEM((cx, cz), f32),
            pltpu.VMEM((cx, cz), f32),
            pltpu.VMEM((reach, 4 * wells, slots), f32),
            pltpu.VMEM((4, rows, slots), f32),
            pltpu.VMEM((rows, slots), jnp.int32),
            pltpu.VMEM((rows * slots, 2 * cz), jnp.bfloat16),
            pltpu.VMEM((SWEEPS, rows, slots), f32),
            pltpu.VMEM((SWEEPS, peers, rows, slots), f32),
            pltpu.SemaphoreType.DMA((reach + 1,)),
            pltpu.SemaphoreType.DMA((reach + 1,)),
            pltpu.SemaphoreType.DMA((SWEEPS, 4)),
            pltpu.SemaphoreType.DMA((SWEEPS, 4)),
            pltpu.SemaphoreType.DMA((SWEEPS, peers)),
            pltpu.SemaphoreType.DMA((SWEEPS, peers)),
        ],
        compiler_params=pltpu.CompilerParams(
            collective_id=0, has_side_effects=True, vmem_limit_bytes=60 * 1024 * 1024
        ),
    )(*args)


def solution(mesh):
    return jax.shard_map(
        shards,
        mesh=mesh,
        in_specs=(P("gx", "gy", None),) * 5
        + (P(None, "gx", "gy", None),)
        + (P("gx", "gy", None),) * 4,
        out_specs=(P("gx", "gy", None), P("gx", "gy", None)),
        check_vma=False,
    )
```

```python
import functools

import jax
import jax.numpy as jnp
from jax import lax
from jax.experimental import pallas as pl
from jax.experimental.pallas import tpu as pltpu
from jax.sharding import PartitionSpec as P

SWEEPS = 6
MESH = pl.DeviceIdType.MESH
WEST, EAST, SOUTH, NORTH = range(4)
C_W, C_E, C_S, C_N, C_EDGE, C_D, C_U, C_INV, C_RHS = range(9)


def kernel(
    reach,
    rhs_hbm,
    acc_hbm,
    tx_hbm,
    ty_hbm,
    tz_hbm,
    held_hbm,
    host_hbm,
    wi_hbm,
    sc_hbm,
    sr_hbm,
    p_hbm,
    s_hbm,
    rhs_ref,
    acc_ref,
    tx_ref,
    ty_ref,
    tz_ref,
    held_ref,
    host_ref,
    wi_ref,
    sc_ref,
    sr_ref,
    fetch_sem,
    s_out,
    out_sem,
    p_buf,
    halo,
    y_stage,
    coef,
    tx_halo,
    ty_halo,
    ty_stage,
    packs,
    params,
    held_buf,
    slot_column,
    cell_buf,
    cell_recv,
    init_send,
    init_recv,
    halo_send,
    halo_recv,
    cell_send,
    cell_rsem,
):
    cx, cy, cz = rhs_ref.shape
    wells = wi_ref.shape[1]
    rows = reach * wells
    gx, gy = lax.axis_index("gx"), lax.axis_index("gy")
    nx, ny = lax.axis_size("gx"), lax.axis_size("gy")
    has_w, has_e = gx > 0, gx < nx - 1
    has_s, has_n = gy > 0, gy < ny - 1
    offsets = [d for d in range(1 - reach, reach) if d != 0]
    index_of = {d: i for i, d in enumerate(offsets)}

    def along_x(d):
        return {"gx": lax.rem(gx + d + nx, nx)}

    def send(src, dst, ssem, rsem, device):
        return pltpu.make_async_remote_copy(
            src_ref=src,
            dst_ref=dst,
            send_sem=ssem,
            recv_sem=rsem,
            device_id=device,
            device_id_type=MESH,
        )

    zero = jnp.zeros((cy, cz), jnp.float32)
    for t in range(SWEEPS):
        for side in range(4):
            halo[t, side] = zero
    tx_halo[...] = zero
    ty_halo[...] = zero

    barrier = pltpu.get_barrier_semaphore()
    for d in offsets:
        pl.semaphore_signal(barrier, inc=1, device_id=along_x(d), device_id_type=MESH)

    @pl.when(has_s)
    def _():
        pl.semaphore_signal(barrier, inc=1, device_id={"gy": gy - 1}, device_id_type=MESH)

    @pl.when(has_n)
    def _():
        pl.semaphore_signal(barrier, inc=1, device_id={"gy": gy + 1}, device_id_type=MESH)

    fetches = [
        pltpu.make_async_copy(src, dst, fetch_sem.at[i])
        for i, (src, dst) in enumerate(
            (
                (host_hbm, host_ref),
                (wi_hbm, wi_ref),
                (sc_hbm, sc_ref),
                (sr_hbm, sr_ref),
                (ty_hbm, ty_ref),
                (tx_hbm, tx_ref),
                (held_hbm, held_ref),
                (acc_hbm, acc_ref),
                (tz_hbm, tz_ref),
                (rhs_hbm, rhs_ref),
            )
        )
    ]
    for fetch in fetches:
        fetch.start()
    for fetch in fetches[:6]:
        fetch.wait()
    packs[0, 0:wells] = host_ref[0].astype(jnp.float32)
    packs[0, wells : 2 * wells] = wi_ref[0]
    packs[0, 2 * wells : 3 * wells] = sc_ref[0]
    packs[0, 3 * wells : 4 * wells] = sr_ref[0]
    ty_stage[...] = ty_ref[:, cy - 1, :]
    pl.semaphore_wait(
        barrier, len(offsets) + has_s.astype(jnp.int32) + has_n.astype(jnp.int32)
    )

    def pack_copy(d):
        return send(
            packs.at[0], packs.at[d], init_send.at[d], init_recv.at[d], along_x(d)
        )

    def tx_copy():
        return send(
            tx_ref.at[cx - 1], tx_halo, init_send.at[0], init_recv.at[0], along_x(1)
        )

    def ty_copy():
        return send(
            ty_stage, ty_halo, init_send.at[reach], init_recv.at[reach], {"gy": gy + 1}
        )

    for d in range(reach - 1, 0, -1):
        pack_copy(d).start()
    pl.when(has_e)(lambda: tx_copy().start())
    pl.when(has_n)(lambda: ty_copy().start())

    for fetch in fetches[6:]:
        fetch.wait()

    for r in range(reach):
        held_buf[r * wells : (r + 1) * wells] = held_ref[r, 0]
    held = held_buf[...]
    row_of = held // cz
    z_of = held - row_of * cz
    lines = cx * cy // 2
    half_of = row_of // lines
    line_of = row_of - half_of * lines
    column_of = half_of * cz + z_of
    column_iota = lax.broadcasted_iota(jnp.int32, (2 * cz, cz), 0)
    for s in range(rows):
        column = jnp.broadcast_to(column_of[s : s + 1, :], column_iota.shape)
        hit = (column_iota == column).astype(jnp.float32)
        slot_column[s * cz : (s + 1) * cz, :] = hit.T.astype(jnp.bfloat16)
    line_iota = lax.broadcasted_iota(jnp.int32, (lines, cz), 0)

    lane = lax.broadcasted_iota(jnp.int32, (cy, cz), 1)
    sub = lax.broadcasted_iota(jnp.int32, (cy, cz), 0)
    level = (lax.broadcasted_iota(jnp.int32, (rows, cz), 0) // wells).astype(jnp.float32)

    def gather(t):
        found = []
        for x in range(cx):
            cell_p = jnp.zeros((rows, cz), jnp.float32)
            for y in range(cy):
                line = jnp.broadcast_to(p_buf[t, x, pl.ds(y, 1), :], (rows, cz))
                got = jnp.take_along_axis(line, z_of, axis=1, mode="promise_in_bounds")
                cell_p = jnp.where(row_of == x * cy + y, got, cell_p)
            found.append(cell_p)
        while len(found) > 1:
            found = [sum(found[i : i + 2]) for i in range(0, len(found), 2)]
        return found[0]

    def scatter(flux):
        high = flux.astype(jnp.bfloat16).astype(jnp.float32)
        rest = flux - high
        mid = rest.astype(jnp.bfloat16).astype(jnp.float32)
        low = rest - mid
        pieces = []
        for s in range(rows):
            at_line = line_iota == jnp.broadcast_to(line_of[s : s + 1, :], line_iota.shape)
            pieces.append(
                jnp.concatenate(
                    [
                        jnp.where(at_line, jnp.broadcast_to(part[s : s + 1, :], at_line.shape), 0.0)
                        for part in (high, mid, low)
                    ],
                    axis=0,
                ).astype(jnp.bfloat16)
            )
        spread = jnp.dot(
            jnp.concatenate(pieces, axis=1), slot_column[...], preferred_element_type=jnp.float32
        )
        spread = spread[:lines] + spread[lines : 2 * lines] + spread[2 * lines :]
        return [
            spread[x % (cx // 2) * cy :][:cy, x // (cx // 2) * cz :][:, :cz] for x in range(cx)
        ]

    def halo_copies(t):
        return (
            (has_w, send(p_buf.at[t, 0], halo.at[t, EAST], halo_send.at[t, WEST],
                         halo_recv.at[t, EAST], {"gx": gx - 1})),
            (has_e, send(p_buf.at[t, cx - 1], halo.at[t, WEST], halo_send.at[t, EAST],
                         halo_recv.at[t, WEST], {"gx": gx + 1})),
            (has_s, send(y_stage.at[t, 0], halo.at[t, NORTH], halo_send.at[t, SOUTH],
                         halo_recv.at[t, NORTH], {"gy": gy - 1})),
            (has_n, send(y_stage.at[t, 1], halo.at[t, SOUTH], halo_send.at[t, NORTH],
                         halo_recv.at[t, SOUTH], {"gy": gy + 1})),
        )

    def send_x(t):
        for there, copy in halo_copies(t)[:2]:
            pl.when(there)(copy.start)

    def send_y(t):
        y_stage[t, 0] = p_buf[t, :, 0, :]
        y_stage[t, 1] = p_buf[t, :, cy - 1, :]
        for there, copy in halo_copies(t)[2:]:
            pl.when(there)(copy.start)

    def wait_halo(t, side):
        there = (has_w, has_e, has_s, has_n)[side]
        copy = send(halo.at[t, side], halo.at[t, side], halo_send.at[t, side],
                    halo_recv.at[t, side], along_x(1))
        pl.when(there)(copy.wait_recv)

    def all_cells(t):
        return send(cell_recv.at[t], cell_recv.at[t], cell_send.at[t], cell_rsem.at[t], along_x(1))

    def drain(t):
        for there, copy in halo_copies(t):
            pl.when(there)(copy.wait_send)
        all_cells(t).wait_send()

    def cell_copy(t, d):
        return send(cell_buf.at[t], cell_recv.at[t, index_of[-d]],
                    cell_send.at[t], cell_rsem.at[t], along_x(d))

    def merge(t):
        cell_p = cell_buf[t]
        all_cells(t).wait_recv()
        for d in offsets:
            got = pltpu.roll(cell_recv[t, index_of[d]], (-d * wells) % rows, 0)
            cell_p = jnp.where(host == level + d, got, cell_p)
        return cell_p

    def well_step(seg, cell_p):
        before = pltpu.roll(seg, 1, 1)
        after = pltpu.roll(seg, cz - 1, 1)
        return 0.2 * seg + seg_inv * (rate + wi * cell_p + fm * before + fp * after)

    def grid_step(t, well_term, more):
        parts = []
        for x in range(cx):
            p = p_buf[t, x]
            total = 0.3 * p + coef[C_RHS, x] - coef[C_INV, x] * well_term[x]
            total += coef[C_U, x] * pltpu.roll(p, cz - 1, 1) + coef[C_D, x] * pltpu.roll(p, 1, 1)
            total += coef[C_N, x] * pltpu.roll(p, cy - 1, 0) + coef[C_S, x] * pltpu.roll(p, 1, 0)
            if x > 0:
                total += coef[C_W, x] * p_buf[t, x - 1]
            if x < cx - 1:
                total += coef[C_E, x] * p_buf[t, x + 1]
            parts.append(total)
        wait_halo(t, SOUTH)
        wait_halo(t, NORTH)
        for x in range(cx):
            north = jnp.broadcast_to(halo[t, NORTH, pl.ds(x, 1), :], (cy, cz))
            south = jnp.broadcast_to(halo[t, SOUTH, pl.ds(x, 1), :], (cy, cz))
            parts[x] += coef[C_EDGE, x] * jnp.where(sub == 0, south, north)
            if 0 < x < cx - 1:
                p_buf[t + 1, x] = parts[x]
        copies = halo_copies(t + 1) if more else None
        for side, x, at in ((WEST, 0, C_W), (EAST, cx - 1, C_E)):
            wait_halo(t, side)
            p_buf[t + 1, x] = parts[x] + coef[at, x] * halo[t, side]
            if more:
                pl.when(copies[side][0])(copies[side][1].start)
        if more:
            send_y(t + 1)

    pl.when(has_w)(tx_copy().wait_recv)
    pl.when(has_s)(ty_copy().wait_recv)
    for x in range(cx):
        ex, ey, ez = tx_ref[x], ty_ref[x], tz_ref[x]
        wx = tx_halo[...] if x == 0 else tx_ref[x - 1]
        edge_y = jnp.broadcast_to(ty_halo[pl.ds(x, 1), :], (cy, cz))
        wy = jnp.where(sub == 0, edge_y, pltpu.roll(ey, 1, 0))
        wz = jnp.where(lane == 0, 0.0, pltpu.roll(ez, 1, 1))
        diag = acc_ref[x] + ex + wx + ey + wy + ez + wz
        inv = 0.7 / diag
        coef[C_W, x] = inv * wx
        coef[C_E, x] = inv * ex
        coef[C_S, x] = jnp.where(sub == 0, 0.0, inv * wy)
        coef[C_N, x] = jnp.where(sub == cy - 1, 0.0, inv * ey)
        coef[C_EDGE, x] = jnp.where(
            sub == 0, inv * wy, jnp.where(sub == cy - 1, inv * ey, 0.0)
        )
        coef[C_D, x] = inv * wz
        coef[C_U, x] = jnp.where(lane == cz - 1, 0.0, inv * ez)
        coef[C_INV, x] = inv
        coef[C_RHS, x] = inv * rhs_ref[x]

    for d in range(1, reach):
        pack_copy(d).wait_recv()
    for r in range(reach):
        for k in range(4):
            params[k, r * wells : (r + 1) * wells] = packs[r, k * wells : (k + 1) * wells]
    host = params[0]
    wi = params[1]
    rate = params[3]
    slot = lax.broadcasted_iota(jnp.int32, (rows, cz), 1)
    fm = jnp.where(slot > 0, params[2], 0.0)
    fp = jnp.where(slot < cz - 1, pltpu.roll(fm, cz - 1, 1), 0.0)
    seg_inv = 0.8 / (wi + fm + fp)
    mine = host == level

    seg = seg_inv * rate
    well_term = scatter(jnp.where(mine, -wi * seg, 0.0))
    for x in range(cx):
        p_buf[1, x] = coef[C_RHS, x] - coef[C_INV, x] * well_term[x]
    send_x(1)
    send_y(1)

    def sweep(t, seg, first):
        cell_p = gather(t)
        cell_buf[t] = cell_p
        for d in offsets:
            cell_copy(t, d).start()
        if not first:
            seg = well_step(seg, merge(t - 1))
        flux = wi * (cell_p - well_step(seg, cell_p))
        well_term = scatter(jnp.where(mine, flux, 0.0))
        return seg, well_term

    def middle(t, seg, first):
        seg, well_term = sweep(t, seg, first)
        if not first:
            drain(t - 1)
        grid_step(t, well_term, True)
        return seg

    seg = middle(1, seg, True)
    seg = lax.fori_loop(2, SWEEPS - 1, lambda t, seg: middle(t, seg, False), seg)
    last = SWEEPS - 1
    seg, well_term = sweep(last, seg, False)
    drain(last - 1)
    grid_step(last, well_term, False)
    p_copy = pltpu.make_async_copy(p_buf.at[SWEEPS], p_hbm, out_sem.at[0])
    p_copy.start()
    for d in range(1, reach):
        pack_copy(d).wait_send()
    pl.when(has_e)(lambda: tx_copy().wait_send())
    pl.when(has_n)(lambda: ty_copy().wait_send())
    drain(last)
    seg = well_step(seg, merge(last))
    s_out[0] = seg[:wells]
    s_copy = pltpu.make_async_copy(s_out, s_hbm, out_sem.at[1])
    s_copy.start()
    p_copy.wait()
    s_copy.wait()


def shards(*args):
    rhs, acc, tx, ty, tz, held, host, wi, sc, sr = args
    reach = held.shape[0]
    wells, slots = wi.shape[1:]
    rows = reach * wells
    cx, cy, cz = rhs.shape
    peers = 2 * (reach - 1)
    hbm = pl.BlockSpec(memory_space=pltpu.HBM)
    f32 = jnp.float32
    return pl.pallas_call(
        functools.partial(kernel, reach),
        out_shape=(
            jax.ShapeDtypeStruct(rhs.shape, f32),
            jax.ShapeDtypeStruct(sr.shape, f32),
        ),
        in_specs=[hbm] * 10,
        out_specs=(hbm, hbm),
        scratch_shapes=[pltpu.VMEM(a.shape, a.dtype) for a in args]
        + [
            pltpu.SemaphoreType.DMA((len(args),)),
            pltpu.VMEM(sr.shape, f32),
            pltpu.SemaphoreType.DMA((2,)),
            pltpu.VMEM((SWEEPS + 1, cx, cy, cz), f32),
            pltpu.VMEM((SWEEPS, 4, cy, cz), f32),
            pltpu.VMEM((SWEEPS, 2, cx, cz), f32),
            pltpu.VMEM((9, cx, cy, cz), f32),
            pltpu.VMEM((cy, cz), f32),
            pltpu.VMEM((cx, cz), f32),
            pltpu.VMEM((cx, cz), f32),
            pltpu.VMEM((reach, 4 * wells, slots), f32),
            pltpu.VMEM((4, rows, slots), f32),
            pltpu.VMEM((rows, slots), jnp.int32),
            pltpu.VMEM((rows * slots, 2 * cz), jnp.bfloat16),
            pltpu.VMEM((SWEEPS, rows, slots), f32),
            pltpu.VMEM((SWEEPS, peers, rows, slots), f32),
            pltpu.SemaphoreType.DMA((reach + 1,)),
            pltpu.SemaphoreType.DMA((reach + 1,)),
            pltpu.SemaphoreType.DMA((SWEEPS, 4)),
            pltpu.SemaphoreType.DMA((SWEEPS, 4)),
            pltpu.SemaphoreType.DMA((SWEEPS,)),
            pltpu.SemaphoreType.DMA((SWEEPS,)),
        ],
        compiler_params=pltpu.CompilerParams(
            collective_id=0, has_side_effects=True, vmem_limit_bytes=60 * 1024 * 1024
        ),
    )(*args)


def solution(mesh):
    return jax.shard_map(
        shards,
        mesh=mesh,
        in_specs=(P("gx", "gy", None),) * 5
        + (P(None, "gx", "gy", None),)
        + (P("gx", "gy", None),) * 4,
        out_specs=(P("gx", "gy", None), P("gx", "gy", None)),
        check_vma=False,
    )
```

```python
import functools

import jax
import jax.numpy as jnp
from jax import lax
from jax.experimental import pallas as pl
from jax.experimental.pallas import tpu as pltpu
from jax.sharding import PartitionSpec as P

SWEEPS = 6
MESH = pl.DeviceIdType.MESH
WEST, EAST, SOUTH, NORTH = range(4)
C_W, C_E, C_S, C_N, C_EDGE, C_D, C_U, C_INV, C_RHS = range(9)


def kernel(
    reach,
    rhs_hbm,
    acc_hbm,
    tx_hbm,
    ty_hbm,
    tz_hbm,
    held_hbm,
    host_hbm,
    wi_hbm,
    sc_hbm,
    sr_hbm,
    p_hbm,
    s_hbm,
    rhs_ref,
    acc_ref,
    tx_ref,
    ty_ref,
    tz_ref,
    held_ref,
    host_ref,
    wi_ref,
    sc_ref,
    sr_ref,
    fetch_sem,
    s_out,
    out_sem,
    p_buf,
    halo,
    y_stage,
    coef,
    tx_halo,
    ty_halo,
    ty_stage,
    packs,
    params,
    held_buf,
    slot_column,
    cell_buf,
    cell_recv,
    init_send,
    init_recv,
    halo_send,
    halo_recv,
    cell_send,
    cell_rsem,
):
    cx, cy, cz = rhs_ref.shape
    wells = wi_ref.shape[1]
    rows = reach * wells
    gx, gy = lax.axis_index("gx"), lax.axis_index("gy")
    nx, ny = lax.axis_size("gx"), lax.axis_size("gy")
    has_w, has_e = gx > 0, gx < nx - 1
    has_s, has_n = gy > 0, gy < ny - 1
    offsets = [d for d in range(1 - reach, reach) if d != 0]
    index_of = {d: i for i, d in enumerate(offsets)}

    def along_x(d):
        return {"gx": lax.rem(gx + d + nx, nx)}

    def send(src, dst, ssem, rsem, device):
        return pltpu.make_async_remote_copy(
            src_ref=src,
            dst_ref=dst,
            send_sem=ssem,
            recv_sem=rsem,
            device_id=device,
            device_id_type=MESH,
        )

    def partner(axis, at, other, at_other, step, there):
        inside = there.astype(jnp.int32)
        return {
            axis: at + step * inside,
            other: at_other + (1 - inside) * (1 - 2 * lax.rem(at_other, 2)),
        }

    partners = (
        partner("gx", gx, "gy", gy, -1, has_w),
        partner("gx", gx, "gy", gy, 1, has_e),
        partner("gy", gy, "gx", gx, -1, has_s),
        partner("gy", gy, "gx", gx, 1, has_n),
    )

    zero = jnp.zeros((cy, cz), jnp.float32)
    tx_halo[...] = zero
    ty_halo[...] = zero

    barrier = pltpu.get_barrier_semaphore()
    for d in offsets:
        pl.semaphore_signal(barrier, inc=1, device_id=along_x(d), device_id_type=MESH)

    for device in partners:
        pl.semaphore_signal(barrier, inc=1, device_id=device, device_id_type=MESH)

    fetches = [
        pltpu.make_async_copy(src, dst, fetch_sem.at[i])
        for i, (src, dst) in enumerate(
            (
                (host_hbm, host_ref),
                (wi_hbm, wi_ref),
                (sc_hbm, sc_ref),
                (sr_hbm, sr_ref),
                (ty_hbm, ty_ref),
                (tx_hbm, tx_ref),
                (held_hbm, held_ref),
                (acc_hbm, acc_ref),
                (tz_hbm, tz_ref),
                (rhs_hbm, rhs_ref),
            )
        )
    ]
    for fetch in fetches:
        fetch.start()
    for fetch in fetches[:6]:
        fetch.wait()
    packs[0, 0:wells] = host_ref[0].astype(jnp.float32)
    packs[0, wells : 2 * wells] = wi_ref[0]
    packs[0, 2 * wells : 3 * wells] = sc_ref[0]
    packs[0, 3 * wells : 4 * wells] = sr_ref[0]
    ty_stage[...] = ty_ref[:, cy - 1, :]
    pl.semaphore_wait(barrier, len(offsets) + len(partners))

    def pack_copy(d):
        return send(
            packs.at[0], packs.at[d], init_send.at[d], init_recv.at[d], along_x(d)
        )

    def tx_copy():
        return send(
            tx_ref.at[cx - 1], tx_halo, init_send.at[0], init_recv.at[0], along_x(1)
        )

    def ty_copy():
        return send(
            ty_stage, ty_halo, init_send.at[reach], init_recv.at[reach], {"gy": gy + 1}
        )

    for d in range(reach - 1, 0, -1):
        pack_copy(d).start()
    pl.when(has_e)(lambda: tx_copy().start())
    pl.when(has_n)(lambda: ty_copy().start())

    for fetch in fetches[6:]:
        fetch.wait()

    for r in range(reach):
        held_buf[r * wells : (r + 1) * wells] = held_ref[r, 0]
    held = held_buf[...]
    row_of = held // cz
    z_of = held - row_of * cz
    lines = cx * cy // 2
    half_of = row_of // lines
    line_of = row_of - half_of * lines
    column_of = half_of * cz + z_of
    column_iota = lax.broadcasted_iota(jnp.int32, (2 * cz, cz), 0)
    for s in range(rows):
        column = jnp.broadcast_to(column_of[s : s + 1, :], column_iota.shape)
        hit = (column_iota == column).astype(jnp.float32)
        slot_column[s * cz : (s + 1) * cz, :] = hit.T.astype(jnp.bfloat16)
    line_iota = lax.broadcasted_iota(jnp.int32, (lines, cz), 0)

    lane = lax.broadcasted_iota(jnp.int32, (cy, cz), 1)
    sub = lax.broadcasted_iota(jnp.int32, (cy, cz), 0)
    level = (lax.broadcasted_iota(jnp.int32, (rows, cz), 0) // wells).astype(jnp.float32)

    def gather(t):
        found = []
        for x in range(cx):
            cell_p = jnp.zeros((rows, cz), jnp.float32)
            for y in range(cy):
                line = jnp.broadcast_to(p_buf[t, x, pl.ds(y, 1), :], (rows, cz))
                got = jnp.take_along_axis(line, z_of, axis=1, mode="promise_in_bounds")
                cell_p = jnp.where(row_of == x * cy + y, got, cell_p)
            found.append(cell_p)
        while len(found) > 1:
            found = [sum(found[i : i + 2]) for i in range(0, len(found), 2)]
        return found[0]

    def scatter(flux):
        high = flux.astype(jnp.bfloat16).astype(jnp.float32)
        rest = flux - high
        mid = rest.astype(jnp.bfloat16).astype(jnp.float32)
        low = rest - mid
        pieces = []
        for s in range(rows):
            at_line = line_iota == jnp.broadcast_to(line_of[s : s + 1, :], line_iota.shape)
            pieces.append(
                jnp.concatenate(
                    [
                        jnp.where(at_line, jnp.broadcast_to(part[s : s + 1, :], at_line.shape), 0.0)
                        for part in (high, mid, low)
                    ],
                    axis=0,
                ).astype(jnp.bfloat16)
            )
        spread = jnp.dot(
            jnp.concatenate(pieces, axis=1), slot_column[...], preferred_element_type=jnp.float32
        )
        spread = spread[:lines] + spread[lines : 2 * lines] + spread[2 * lines :]
        return [
            spread[x % (cx // 2) * cy :][:cy, x // (cx // 2) * cz :][:, :cz] for x in range(cx)
        ]

    def halo_copy(t, side):
        src = (p_buf.at[t, 0], p_buf.at[t, cx - 1], y_stage.at[t, 0], y_stage.at[t, 1])[side]
        there = (has_w, has_e, has_s, has_n)[side].astype(jnp.int32)
        opposite = (EAST, WEST, NORTH, SOUTH)[side]
        lands = side + (opposite - side) * there
        return send(src, halo.at[t, lands], halo_send.at[t], halo_recv.at[t, lands],
                    partners[side])

    def send_x(t):
        halo_copy(t, WEST).start()
        halo_copy(t, EAST).start()

    def send_y(t):
        y_stage[t, 0] = p_buf[t, :, 0, :]
        y_stage[t, 1] = p_buf[t, :, cy - 1, :]
        halo_copy(t, SOUTH).start()
        halo_copy(t, NORTH).start()

    def wait_halo(t, side):
        send(halo.at[t, side], halo.at[t, side], halo_send.at[t],
             halo_recv.at[t, side], partners[side]).wait_recv()

    def all_cells(t):
        return send(cell_recv.at[t], cell_recv.at[t], cell_send.at[t], cell_rsem.at[t], along_x(1))

    def drain(t):
        send(halo.at[t], halo.at[t], halo_send.at[t], halo_recv.at[t, 0], partners[0]).wait_send()
        all_cells(t).wait_send()

    def cell_copy(t, d):
        return send(cell_buf.at[t], cell_recv.at[t, index_of[-d]],
                    cell_send.at[t], cell_rsem.at[t], along_x(d))

    def merge(t):
        cell_p = cell_buf[t]
        all_cells(t).wait_recv()
        for d in offsets:
            got = pltpu.roll(cell_recv[t, index_of[d]], (-d * wells) % rows, 0)
            cell_p = jnp.where(host == level + d, got, cell_p)
        return cell_p

    def well_step(seg, cell_p):
        before = pltpu.roll(seg, 1, 1)
        after = pltpu.roll(seg, cz - 1, 1)
        return 0.2 * seg + seg_inv * (rate + wi * cell_p + fm * before + fp * after)

    def grid_step(t, well_term, more):
        parts = []
        for x in range(cx):
            p = p_buf[t, x]
            total = 0.3 * p + coef[C_RHS, x] - coef[C_INV, x] * well_term[x]
            total += coef[C_U, x] * pltpu.roll(p, cz - 1, 1) + coef[C_D, x] * pltpu.roll(p, 1, 1)
            total += coef[C_N, x] * pltpu.roll(p, cy - 1, 0) + coef[C_S, x] * pltpu.roll(p, 1, 0)
            if x > 0:
                total += coef[C_W, x] * p_buf[t, x - 1]
            if x < cx - 1:
                total += coef[C_E, x] * p_buf[t, x + 1]
            parts.append(total)
        wait_halo(t, SOUTH)
        wait_halo(t, NORTH)
        for x in range(cx):
            north = jnp.broadcast_to(halo[t, NORTH, pl.ds(x, 1), :], (cy, cz))
            south = jnp.broadcast_to(halo[t, SOUTH, pl.ds(x, 1), :], (cy, cz))
            parts[x] += coef[C_EDGE, x] * jnp.where(sub == 0, south, north)
            if 0 < x < cx - 1:
                p_buf[t + 1, x] = parts[x]
        for side, x, at in ((WEST, 0, C_W), (EAST, cx - 1, C_E)):
            wait_halo(t, side)
            p_buf[t + 1, x] = parts[x] + coef[at, x] * halo[t, side]
            if more:
                halo_copy(t + 1, side).start()
        if more:
            send_y(t + 1)

    pl.when(has_w)(tx_copy().wait_recv)
    pl.when(has_s)(ty_copy().wait_recv)
    for x in range(cx):
        ex, ey, ez = tx_ref[x], ty_ref[x], tz_ref[x]
        wx = tx_halo[...] if x == 0 else tx_ref[x - 1]
        edge_y = jnp.broadcast_to(ty_halo[pl.ds(x, 1), :], (cy, cz))
        wy = jnp.where(sub == 0, edge_y, pltpu.roll(ey, 1, 0))
        wz = jnp.where(lane == 0, 0.0, pltpu.roll(ez, 1, 1))
        diag = acc_ref[x] + ex + wx + ey + wy + ez + wz
        inv = 0.7 / diag
        coef[C_W, x] = inv * wx
        coef[C_E, x] = jnp.where(has_e, inv * ex, 0.0) if x == cx - 1 else inv * ex
        coef[C_S, x] = jnp.where(sub == 0, 0.0, inv * wy)
        coef[C_N, x] = jnp.where(sub == cy - 1, 0.0, inv * ey)
        coef[C_EDGE, x] = jnp.where(
            sub == 0, inv * wy, jnp.where((sub == cy - 1) & has_n, inv * ey, 0.0)
        )
        coef[C_D, x] = inv * wz
        coef[C_U, x] = jnp.where(lane == cz - 1, 0.0, inv * ez)
        coef[C_INV, x] = inv
        coef[C_RHS, x] = inv * rhs_ref[x]

    for d in range(1, reach):
        pack_copy(d).wait_recv()
    for r in range(reach):
        for k in range(4):
            params[k, r * wells : (r + 1) * wells] = packs[r, k * wells : (k + 1) * wells]
    host = params[0]
    wi = params[1]
    rate = params[3]
    slot = lax.broadcasted_iota(jnp.int32, (rows, cz), 1)
    fm = jnp.where(slot > 0, params[2], 0.0)
    fp = jnp.where(slot < cz - 1, pltpu.roll(fm, cz - 1, 1), 0.0)
    seg_inv = 0.8 / (wi + fm + fp)
    mine = host == level

    seg = seg_inv * rate
    well_term = scatter(jnp.where(mine, -wi * seg, 0.0))
    for x in range(cx):
        p_buf[1, x] = coef[C_RHS, x] - coef[C_INV, x] * well_term[x]
    send_x(1)
    send_y(1)

    def sweep(t, seg, first):
        cell_p = gather(t)
        cell_buf[t] = cell_p
        for d in offsets:
            cell_copy(t, d).start()
        if not first:
            seg = well_step(seg, merge(t - 1))
        flux = wi * (cell_p - well_step(seg, cell_p))
        well_term = scatter(jnp.where(mine, flux, 0.0))
        return seg, well_term

    def middle(t, seg, first):
        seg, well_term = sweep(t, seg, first)
        if not first:
            drain(t - 1)
        grid_step(t, well_term, True)
        return seg

    seg = middle(1, seg, True)
    seg = lax.fori_loop(2, SWEEPS - 1, lambda t, seg: middle(t, seg, False), seg)
    last = SWEEPS - 1
    seg, well_term = sweep(last, seg, False)
    drain(last - 1)
    grid_step(last, well_term, False)
    p_copy = pltpu.make_async_copy(p_buf.at[SWEEPS], p_hbm, out_sem.at[0])
    p_copy.start()
    for d in range(1, reach):
        pack_copy(d).wait_send()
    pl.when(has_e)(lambda: tx_copy().wait_send())
    pl.when(has_n)(lambda: ty_copy().wait_send())
    drain(last)
    seg = well_step(seg, merge(last))
    s_out[0] = seg[:wells]
    s_copy = pltpu.make_async_copy(s_out, s_hbm, out_sem.at[1])
    s_copy.start()
    p_copy.wait()
    s_copy.wait()


def hand_out(p_in, s_in, p_out, s_out, sems):
    copies = (
        pltpu.make_async_copy(p_in, p_out, sems.at[0]),
        pltpu.make_async_copy(s_in, s_out, sems.at[1]),
    )
    for copy in copies:
        copy.start()
    for copy in copies:
        copy.wait()


def shards(*args):
    rhs, acc, tx, ty, tz, held, host, wi, sc, sr = args
    reach = held.shape[0]
    wells, slots = wi.shape[1:]
    rows = reach * wells
    cx, cy, cz = rhs.shape
    peers = 2 * (reach - 1)
    hbm = pl.BlockSpec(memory_space=pltpu.HBM)
    f32 = jnp.float32
    shapes = (jax.ShapeDtypeStruct(rhs.shape, f32), jax.ShapeDtypeStruct(sr.shape, f32))
    swept = pl.pallas_call(
        functools.partial(kernel, reach),
        out_shape=shapes,
        in_specs=[hbm] * 10,
        out_specs=(hbm, hbm),
        scratch_shapes=[pltpu.VMEM(a.shape, a.dtype) for a in args]
        + [
            pltpu.SemaphoreType.DMA((len(args),)),
            pltpu.VMEM(sr.shape, f32),
            pltpu.SemaphoreType.DMA((2,)),
            pltpu.VMEM((SWEEPS + 1, cx, cy, cz), f32),
            pltpu.VMEM((SWEEPS, 4, cy, cz), f32),
            pltpu.VMEM((SWEEPS, 2, cx, cz), f32),
            pltpu.VMEM((9, cx, cy, cz), f32),
            pltpu.VMEM((cy, cz), f32),
            pltpu.VMEM((cx, cz), f32),
            pltpu.VMEM((cx, cz), f32),
            pltpu.VMEM((reach, 4 * wells, slots), f32),
            pltpu.VMEM((4, rows, slots), f32),
            pltpu.VMEM((rows, slots), jnp.int32),
            pltpu.VMEM((rows * slots, 2 * cz), jnp.bfloat16),
            pltpu.VMEM((SWEEPS, rows, slots), f32),
            pltpu.VMEM((SWEEPS, peers, rows, slots), f32),
            pltpu.SemaphoreType.DMA((reach + 1,)),
            pltpu.SemaphoreType.DMA((reach + 1,)),
            pltpu.SemaphoreType.DMA((SWEEPS,)),
            pltpu.SemaphoreType.DMA((SWEEPS, 4)),
            pltpu.SemaphoreType.DMA((SWEEPS,)),
            pltpu.SemaphoreType.DMA((SWEEPS,)),
        ],
        compiler_params=pltpu.CompilerParams(
            collective_id=0, has_side_effects=True, vmem_limit_bytes=60 * 1024 * 1024
        ),
    )(*args)
    return pl.pallas_call(
        hand_out,
        out_shape=shapes,
        in_specs=[hbm] * 2,
        out_specs=(hbm, hbm),
        scratch_shapes=[pltpu.SemaphoreType.DMA((2,))],
        compiler_params=pltpu.CompilerParams(vmem_limit_bytes=60 * 1024 * 1024),
    )(*swept)


def solution(mesh):
    return jax.shard_map(
        shards,
        mesh=mesh,
        in_specs=(P("gx", "gy", None),) * 5
        + (P(None, "gx", "gy", None),)
        + (P("gx", "gy", None),) * 4,
        out_specs=(P("gx", "gy", None), P("gx", "gy", None)),
        check_vma=False,
    )
```

```python
import functools

import jax
import jax.numpy as jnp
from jax import lax
from jax.experimental import pallas as pl
from jax.experimental.pallas import tpu as pltpu
from jax.sharding import PartitionSpec as P

SWEEPS = 6
MESH = pl.DeviceIdType.MESH
WEST, EAST, SOUTH, NORTH = range(4)
C_W, C_E, C_S, C_N, C_EDGE, C_D, C_U, C_INV, C_RHS = range(9)


def kernel(
    reach,
    rhs_hbm,
    acc_hbm,
    tx_hbm,
    ty_hbm,
    tz_hbm,
    held_hbm,
    host_hbm,
    wi_hbm,
    sc_hbm,
    sr_hbm,
    p_hbm,
    s_hbm,
    rhs_ref,
    acc_ref,
    tx_ref,
    ty_ref,
    tz_ref,
    held_ref,
    host_ref,
    wi_ref,
    sc_ref,
    sr_ref,
    fetch_sem,
    s_out,
    out_sem,
    p_buf,
    halo,
    y_stage,
    coef,
    tx_halo,
    ty_halo,
    ty_stage,
    packs,
    params,
    held_buf,
    slot_column,
    cell_buf,
    cell_recv,
    init_send,
    init_recv,
    halo_send,
    halo_recv,
    cell_send,
    cell_rsem,
):
    cx, cy, cz = rhs_ref.shape
    wells = wi_ref.shape[1]
    rows = reach * wells
    gx, gy = lax.axis_index("gx"), lax.axis_index("gy")
    nx, ny = lax.axis_size("gx"), lax.axis_size("gy")
    has_w, has_e = gx > 0, gx < nx - 1
    has_s, has_n = gy > 0, gy < ny - 1
    offsets = [d for d in range(1 - reach, reach) if d != 0]
    index_of = {d: i for i, d in enumerate(offsets)}

    def along_x(d):
        return {"gx": lax.rem(gx + d + nx, nx)}

    def send(src, dst, ssem, rsem, device):
        return pltpu.make_async_remote_copy(
            src_ref=src,
            dst_ref=dst,
            send_sem=ssem,
            recv_sem=rsem,
            device_id=device,
            device_id_type=MESH,
        )

    def partner(axis, at, other, at_other, step, there):
        inside = there.astype(jnp.int32)
        return {
            axis: at + step * inside,
            other: at_other + (1 - inside) * (1 - 2 * lax.rem(at_other, 2)),
        }

    partners = (
        partner("gx", gx, "gy", gy, -1, has_w),
        partner("gx", gx, "gy", gy, 1, has_e),
        partner("gy", gy, "gx", gx, -1, has_s),
        partner("gy", gy, "gx", gx, 1, has_n),
    )

    zero = jnp.zeros((cy, cz), jnp.float32)
    tx_halo[...] = zero
    ty_halo[...] = zero

    barrier = pltpu.get_barrier_semaphore()
    for d in offsets:
        pl.semaphore_signal(barrier, inc=1, device_id=along_x(d), device_id_type=MESH)

    for device in partners:
        pl.semaphore_signal(barrier, inc=1, device_id=device, device_id_type=MESH)

    fetches = [
        pltpu.make_async_copy(src, dst, fetch_sem.at[i])
        for i, (src, dst) in enumerate(
            (
                (host_hbm, host_ref),
                (wi_hbm, wi_ref),
                (sc_hbm, sc_ref),
                (sr_hbm, sr_ref),
                (ty_hbm, ty_ref),
                (tx_hbm, tx_ref),
                (held_hbm, held_ref),
                (acc_hbm, acc_ref),
                (tz_hbm, tz_ref),
                (rhs_hbm, rhs_ref),
            )
        )
    ]
    for fetch in fetches:
        fetch.start()
    for fetch in fetches[:6]:
        fetch.wait()
    packs[0, 0:wells] = host_ref[0].astype(jnp.float32)
    packs[0, wells : 2 * wells] = wi_ref[0]
    packs[0, 2 * wells : 3 * wells] = sc_ref[0]
    packs[0, 3 * wells : 4 * wells] = sr_ref[0]
    ty_stage[...] = ty_ref[:, cy - 1, :]
    pl.semaphore_wait(barrier, len(offsets) + len(partners))

    def pack_copy(d):
        return send(
            packs.at[0], packs.at[d], init_send.at[d], init_recv.at[d], along_x(d)
        )

    def tx_copy():
        return send(
            tx_ref.at[cx - 1], tx_halo, init_send.at[0], init_recv.at[0], along_x(1)
        )

    def ty_copy():
        return send(
            ty_stage, ty_halo, init_send.at[reach], init_recv.at[reach], {"gy": gy + 1}
        )

    for d in range(reach - 1, 0, -1):
        pack_copy(d).start()
    pl.when(has_e)(lambda: tx_copy().start())
    pl.when(has_n)(lambda: ty_copy().start())

    for fetch in fetches[6:]:
        fetch.wait()

    for r in range(reach):
        held_buf[r * wells : (r + 1) * wells] = held_ref[r, 0]
    held = held_buf[...]
    row_of = held // cz
    z_of = held - row_of * cz
    lines = cx * cy // 2
    half_of = row_of // lines
    line_of = row_of - half_of * lines
    column_of = half_of * cz + z_of
    column_iota = lax.broadcasted_iota(jnp.int32, (2 * cz, cz), 0)
    for s in range(rows):
        column = jnp.broadcast_to(column_of[s : s + 1, :], column_iota.shape)
        hit = (column_iota == column).astype(jnp.float32)
        slot_column[s * cz : (s + 1) * cz, :] = hit.T.astype(jnp.bfloat16)
    line_iota = lax.broadcasted_iota(jnp.int32, (lines, cz), 0)

    lane = lax.broadcasted_iota(jnp.int32, (cy, cz), 1)
    sub = lax.broadcasted_iota(jnp.int32, (cy, cz), 0)
    level = (lax.broadcasted_iota(jnp.int32, (rows, cz), 0) // wells).astype(jnp.float32)

    def gather(t):
        found = []
        for x in range(cx):
            cell_p = jnp.zeros((rows, cz), jnp.float32)
            for y in range(cy):
                line = jnp.broadcast_to(p_buf[t, x, pl.ds(y, 1), :], (rows, cz))
                got = jnp.take_along_axis(line, z_of, axis=1, mode="promise_in_bounds")
                cell_p = jnp.where(row_of == x * cy + y, got, cell_p)
            found.append(cell_p)
        while len(found) > 1:
            found = [sum(found[i : i + 2]) for i in range(0, len(found), 2)]
        return found[0]

    def scatter(flux):
        high = flux.astype(jnp.bfloat16).astype(jnp.float32)
        rest = flux - high
        mid = rest.astype(jnp.bfloat16).astype(jnp.float32)
        low = rest - mid
        pieces = []
        for s in range(rows):
            at_line = line_iota == jnp.broadcast_to(line_of[s : s + 1, :], line_iota.shape)
            pieces.append(
                jnp.concatenate(
                    [
                        jnp.where(at_line, jnp.broadcast_to(part[s : s + 1, :], at_line.shape), 0.0)
                        for part in (high, mid, low)
                    ],
                    axis=0,
                ).astype(jnp.bfloat16)
            )
        spread = jnp.dot(
            jnp.concatenate(pieces, axis=1), slot_column[...], preferred_element_type=jnp.float32
        )
        spread = spread[:lines] + spread[lines : 2 * lines] + spread[2 * lines :]
        return [
            spread[x % (cx // 2) * cy :][:cy, x // (cx // 2) * cz :][:, :cz] for x in range(cx)
        ]

    def halo_copy(t, side):
        src = (p_buf.at[t, 0], p_buf.at[t, cx - 1], y_stage.at[t, 0], y_stage.at[t, 1])[side]
        there = (has_w, has_e, has_s, has_n)[side].astype(jnp.int32)
        opposite = (EAST, WEST, NORTH, SOUTH)[side]
        lands = side + (opposite - side) * there
        return send(src, halo.at[t, lands], halo_send.at[t], halo_recv.at[t, lands],
                    partners[side])

    def send_x(t):
        halo_copy(t, WEST).start()
        halo_copy(t, EAST).start()

    def send_y(t):
        y_stage[t, 0] = p_buf[t, :, 0, :]
        y_stage[t, 1] = p_buf[t, :, cy - 1, :]
        halo_copy(t, SOUTH).start()
        halo_copy(t, NORTH).start()

    def wait_halo(t, side):
        send(halo.at[t, side], halo.at[t, side], halo_send.at[t],
             halo_recv.at[t, side], partners[side]).wait_recv()

    def all_cells(t):
        return send(cell_recv.at[t], cell_recv.at[t], cell_send.at[t], cell_rsem.at[t], along_x(1))

    def drain(t):
        send(halo.at[t], halo.at[t], halo_send.at[t], halo_recv.at[t, 0], partners[0]).wait_send()
        all_cells(t).wait_send()

    def cell_copy(t, d):
        return send(cell_buf.at[t], cell_recv.at[t, index_of[-d]],
                    cell_send.at[t], cell_rsem.at[t], along_x(d))

    def merge(t):
        cell_p = cell_buf[t]
        all_cells(t).wait_recv()
        for d in offsets:
            got = pltpu.roll(cell_recv[t, index_of[d]], (-d * wells) % rows, 0)
            cell_p = jnp.where(host == level + d, got, cell_p)
        return cell_p

    def well_step(seg, cell_p):
        before = pltpu.roll(seg, 1, 1)
        after = pltpu.roll(seg, cz - 1, 1)
        return 0.2 * seg + seg_inv * (rate + wi * cell_p + fm * before + fp * after)

    def grid_step(t, well_term, more):
        parts = []
        for x in range(cx):
            p = p_buf[t, x]
            total = 0.3 * p + coef[C_RHS, x] - coef[C_INV, x] * well_term[x]
            total += coef[C_U, x] * pltpu.roll(p, cz - 1, 1) + coef[C_D, x] * pltpu.roll(p, 1, 1)
            total += coef[C_N, x] * pltpu.roll(p, cy - 1, 0) + coef[C_S, x] * pltpu.roll(p, 1, 0)
            if x > 0:
                total += coef[C_W, x] * p_buf[t, x - 1]
            if x < cx - 1:
                total += coef[C_E, x] * p_buf[t, x + 1]
            parts.append(total)
        wait_halo(t, SOUTH)
        wait_halo(t, NORTH)
        for x in range(cx):
            north = jnp.broadcast_to(halo[t, NORTH, pl.ds(x, 1), :], (cy, cz))
            south = jnp.broadcast_to(halo[t, SOUTH, pl.ds(x, 1), :], (cy, cz))
            parts[x] += coef[C_EDGE, x] * jnp.where(sub == 0, south, north)
            if 0 < x < cx - 1:
                p_buf[t + 1, x] = parts[x]
        for side, x, at in ((WEST, 0, C_W), (EAST, cx - 1, C_E)):
            wait_halo(t, side)
            p_buf[t + 1, x] = parts[x] + coef[at, x] * halo[t, side]
            if more:
                halo_copy(t + 1, side).start()
        if more:
            send_y(t + 1)

    pl.when(has_w)(tx_copy().wait_recv)
    pl.when(has_s)(ty_copy().wait_recv)
    for x in range(cx):
        ex, ey, ez = tx_ref[x], ty_ref[x], tz_ref[x]
        wx = tx_halo[...] if x == 0 else tx_ref[x - 1]
        edge_y = jnp.broadcast_to(ty_halo[pl.ds(x, 1), :], (cy, cz))
        wy = jnp.where(sub == 0, edge_y, pltpu.roll(ey, 1, 0))
        wz = jnp.where(lane == 0, 0.0, pltpu.roll(ez, 1, 1))
        diag = acc_ref[x] + ex + wx + ey + wy + ez + wz
        inv = 0.7 / diag
        coef[C_W, x] = inv * wx
        coef[C_E, x] = jnp.where(has_e, inv * ex, 0.0) if x == cx - 1 else inv * ex
        coef[C_S, x] = jnp.where(sub == 0, 0.0, inv * wy)
        coef[C_N, x] = jnp.where(sub == cy - 1, 0.0, inv * ey)
        coef[C_EDGE, x] = jnp.where(
            sub == 0, inv * wy, jnp.where((sub == cy - 1) & has_n, inv * ey, 0.0)
        )
        coef[C_D, x] = inv * wz
        coef[C_U, x] = jnp.where(lane == cz - 1, 0.0, inv * ez)
        coef[C_INV, x] = inv
        coef[C_RHS, x] = inv * rhs_ref[x]

    for d in range(1, reach):
        pack_copy(d).wait_recv()
    for r in range(reach):
        for k in range(4):
            params[k, r * wells : (r + 1) * wells] = packs[r, k * wells : (k + 1) * wells]
    host = params[0]
    wi = params[1]
    rate = params[3]
    slot = lax.broadcasted_iota(jnp.int32, (rows, cz), 1)
    fm = jnp.where(slot > 0, params[2], 0.0)
    fp = jnp.where(slot < cz - 1, pltpu.roll(fm, cz - 1, 1), 0.0)
    seg_inv = 0.8 / (wi + fm + fp)
    mine = host == level

    seg = seg_inv * rate
    well_term = scatter(jnp.where(mine, -wi * seg, 0.0))
    for x in range(cx):
        p_buf[1, x] = coef[C_RHS, x] - coef[C_INV, x] * well_term[x]
    send_x(1)
    send_y(1)

    def sweep(t, seg, first):
        cell_p = gather(t)
        cell_buf[t] = cell_p
        for d in offsets:
            cell_copy(t, d).start()
        if not first:
            seg = well_step(seg, merge(t - 1))
        flux = wi * (cell_p - well_step(seg, cell_p))
        well_term = scatter(jnp.where(mine, flux, 0.0))
        return seg, well_term

    def middle(t, seg, first):
        seg, well_term = sweep(t, seg, first)
        if not first:
            drain(t - 1)
        grid_step(t, well_term, True)
        return seg

    seg = middle(1, seg, True)
    seg = lax.fori_loop(2, SWEEPS - 1, lambda t, seg: middle(t, seg, False), seg)
    last = SWEEPS - 1
    seg, well_term = sweep(last, seg, False)
    drain(last - 1)
    grid_step(last, well_term, False)
    p_copy = pltpu.make_async_copy(p_buf.at[SWEEPS], p_hbm, out_sem.at[0])
    p_copy.start()
    for d in range(1, reach):
        pack_copy(d).wait_send()
    pl.when(has_e)(lambda: tx_copy().wait_send())
    pl.when(has_n)(lambda: ty_copy().wait_send())
    drain(last)
    seg = well_step(seg, merge(last))
    s_out[0] = seg[:wells]
    s_copy = pltpu.make_async_copy(s_out, s_hbm, out_sem.at[1])
    s_copy.start()
    p_copy.wait()
    s_copy.wait()


def hand_out(p_in, s_in, p_out, s_out, p_held, s_held, sems):
    arrays = ((p_in, p_held, p_out), (s_in, s_held, s_out))
    inward = [pltpu.make_async_copy(a, b, sems.at[0, i]) for i, (a, b, _) in enumerate(arrays)]
    outward = [pltpu.make_async_copy(b, c, sems.at[1, i]) for i, (_, b, c) in enumerate(arrays)]
    for copy in inward:
        copy.start()
    for fetched, copy in zip(inward, outward):
        fetched.wait()
        copy.start()
    for copy in outward:
        copy.wait()


def shards(*args):
    rhs, acc, tx, ty, tz, held, host, wi, sc, sr = args
    reach = held.shape[0]
    wells, slots = wi.shape[1:]
    rows = reach * wells
    cx, cy, cz = rhs.shape
    peers = 2 * (reach - 1)
    hbm = pl.BlockSpec(memory_space=pltpu.HBM)
    f32 = jnp.float32
    shapes = (jax.ShapeDtypeStruct(rhs.shape, f32), jax.ShapeDtypeStruct(sr.shape, f32))
    swept = pl.pallas_call(
        functools.partial(kernel, reach),
        out_shape=shapes,
        in_specs=[hbm] * 10,
        out_specs=(hbm, hbm),
        scratch_shapes=[pltpu.VMEM(a.shape, a.dtype) for a in args]
        + [
            pltpu.SemaphoreType.DMA((len(args),)),
            pltpu.VMEM(sr.shape, f32),
            pltpu.SemaphoreType.DMA((2,)),
            pltpu.VMEM((SWEEPS + 1, cx, cy, cz), f32),
            pltpu.VMEM((SWEEPS, 4, cy, cz), f32),
            pltpu.VMEM((SWEEPS, 2, cx, cz), f32),
            pltpu.VMEM((9, cx, cy, cz), f32),
            pltpu.VMEM((cy, cz), f32),
            pltpu.VMEM((cx, cz), f32),
            pltpu.VMEM((cx, cz), f32),
            pltpu.VMEM((reach, 4 * wells, slots), f32),
            pltpu.VMEM((4, rows, slots), f32),
            pltpu.VMEM((rows, slots), jnp.int32),
            pltpu.VMEM((rows * slots, 2 * cz), jnp.bfloat16),
            pltpu.VMEM((SWEEPS, rows, slots), f32),
            pltpu.VMEM((SWEEPS, peers, rows, slots), f32),
            pltpu.SemaphoreType.DMA((reach + 1,)),
            pltpu.SemaphoreType.DMA((reach + 1,)),
            pltpu.SemaphoreType.DMA((SWEEPS,)),
            pltpu.SemaphoreType.DMA((SWEEPS, 4)),
            pltpu.SemaphoreType.DMA((SWEEPS,)),
            pltpu.SemaphoreType.DMA((SWEEPS,)),
        ],
        compiler_params=pltpu.CompilerParams(
            collective_id=0, has_side_effects=True, vmem_limit_bytes=60 * 1024 * 1024
        ),
    )(*args)
    return pl.pallas_call(
        hand_out,
        out_shape=shapes,
        in_specs=[hbm] * 2,
        out_specs=(hbm, hbm),
        scratch_shapes=[
            pltpu.VMEM(rhs.shape, f32),
            pltpu.VMEM(sr.shape, f32),
            pltpu.SemaphoreType.DMA((2, 2)),
        ],
        compiler_params=pltpu.CompilerParams(vmem_limit_bytes=60 * 1024 * 1024),
    )(*swept)


def solution(mesh):
    return jax.shard_map(
        shards,
        mesh=mesh,
        in_specs=(P("gx", "gy", None),) * 5
        + (P(None, "gx", "gy", None),)
        + (P("gx", "gy", None),) * 4,
        out_specs=(P("gx", "gy", None), P("gx", "gy", None)),
        check_vma=False,
    )
```

```python
import functools

import jax
import jax.numpy as jnp
from jax import lax
from jax.experimental import pallas as pl
from jax.experimental.pallas import tpu as pltpu
from jax.sharding import PartitionSpec as P

SWEEPS = 6
MESH = pl.DeviceIdType.MESH
WEST, EAST, SOUTH, NORTH = range(4)
C_W, C_E, C_S, C_N, C_EDGE, C_D, C_U, C_INV, C_RHS = range(9)


def kernel(
    reach,
    rhs_hbm,
    acc_hbm,
    tx_hbm,
    ty_hbm,
    tz_hbm,
    held_hbm,
    host_hbm,
    wi_hbm,
    sc_hbm,
    sr_hbm,
    p_hbm,
    s_hbm,
    rhs_ref,
    acc_ref,
    tx_ref,
    ty_ref,
    tz_ref,
    held_ref,
    host_ref,
    wi_ref,
    sc_ref,
    sr_ref,
    fetch_sem,
    s_out,
    out_sem,
    p_buf,
    halo,
    y_stage,
    coef,
    tx_halo,
    ty_halo,
    ty_stage,
    packs,
    params,
    held_buf,
    slot_column,
    cell_buf,
    cell_recv,
    init_send,
    init_recv,
    halo_send,
    halo_recv,
    cell_send,
    cell_rsem,
):
    cx, cy, cz = rhs_ref.shape
    wells = wi_ref.shape[1]
    rows = reach * wells
    gx, gy = lax.axis_index("gx"), lax.axis_index("gy")
    nx, ny = lax.axis_size("gx"), lax.axis_size("gy")
    has_w, has_e = gx > 0, gx < nx - 1
    has_s, has_n = gy > 0, gy < ny - 1
    offsets = [d for d in range(1 - reach, reach) if d != 0]
    index_of = {d: i for i, d in enumerate(offsets)}

    def along_x(d):
        return {"gx": lax.rem(gx + d + nx, nx)}

    def send(src, dst, ssem, rsem, device):
        return pltpu.make_async_remote_copy(
            src_ref=src,
            dst_ref=dst,
            send_sem=ssem,
            recv_sem=rsem,
            device_id=device,
            device_id_type=MESH,
        )

    def partner(axis, at, other, at_other, step, there):
        inside = there.astype(jnp.int32)
        return {
            axis: at + step * inside,
            other: at_other + (1 - inside) * (1 - 2 * lax.rem(at_other, 2)),
        }

    partners = (
        partner("gx", gx, "gy", gy, -1, has_w),
        partner("gx", gx, "gy", gy, 1, has_e),
        partner("gy", gy, "gx", gx, -1, has_s),
        partner("gy", gy, "gx", gx, 1, has_n),
    )

    zero = jnp.zeros((cy, cz), jnp.float32)
    tx_halo[...] = zero
    ty_halo[...] = zero

    barrier = pltpu.get_barrier_semaphore()
    for d in offsets:
        pl.semaphore_signal(barrier, inc=1, device_id=along_x(d), device_id_type=MESH)

    for device in partners:
        pl.semaphore_signal(barrier, inc=1, device_id=device, device_id_type=MESH)

    fetches = [
        pltpu.make_async_copy(src, dst, fetch_sem.at[i])
        for i, (src, dst) in enumerate(
            (
                (host_hbm, host_ref),
                (wi_hbm, wi_ref),
                (sc_hbm, sc_ref),
                (sr_hbm, sr_ref),
                (ty_hbm, ty_ref),
                (tx_hbm, tx_ref),
                (held_hbm, held_ref),
                (acc_hbm, acc_ref),
                (tz_hbm, tz_ref),
                (rhs_hbm, rhs_ref),
            )
        )
    ]
    for fetch in fetches:
        fetch.start()
    for fetch in fetches[:6]:
        fetch.wait()
    packs[0, 0:wells] = host_ref[0].astype(jnp.float32)
    packs[0, wells : 2 * wells] = wi_ref[0]
    packs[0, 2 * wells : 3 * wells] = sc_ref[0]
    packs[0, 3 * wells : 4 * wells] = sr_ref[0]
    ty_stage[...] = ty_ref[:, cy - 1, :]
    pl.semaphore_wait(barrier, len(offsets) + len(partners))

    def pack_copy(d):
        return send(
            packs.at[0], packs.at[d], init_send.at[d], init_recv.at[d], along_x(d)
        )

    def tx_copy():
        return send(
            tx_ref.at[cx - 1], tx_halo, init_send.at[0], init_recv.at[0], along_x(1)
        )

    def ty_copy():
        return send(
            ty_stage, ty_halo, init_send.at[reach], init_recv.at[reach], {"gy": gy + 1}
        )

    for d in range(reach - 1, 0, -1):
        pack_copy(d).start()
    pl.when(has_e)(lambda: tx_copy().start())
    pl.when(has_n)(lambda: ty_copy().start())

    for fetch in fetches[6:]:
        fetch.wait()

    for r in range(reach):
        held_buf[r * wells : (r + 1) * wells] = held_ref[r, 0]
    held = held_buf[...]
    row_of = held // cz
    z_of = held - row_of * cz
    lines = cx * cy // 2
    half_of = row_of // lines
    line_of = row_of - half_of * lines
    column_of = half_of * cz + z_of
    column_iota = lax.broadcasted_iota(jnp.int32, (2 * cz, cz), 0)
    for s in range(rows):
        column = jnp.broadcast_to(column_of[s : s + 1, :], column_iota.shape)
        hit = (column_iota == column).astype(jnp.float32)
        slot_column[s * cz : (s + 1) * cz, :] = hit.T.astype(jnp.bfloat16)
    line_iota = lax.broadcasted_iota(jnp.int32, (lines, cz), 0)

    lane = lax.broadcasted_iota(jnp.int32, (cy, cz), 1)
    sub = lax.broadcasted_iota(jnp.int32, (cy, cz), 0)
    level = (lax.broadcasted_iota(jnp.int32, (rows, cz), 0) // wells).astype(jnp.float32)

    def gather(t):
        found = []
        for x in range(cx):
            cell_p = jnp.zeros((rows, cz), jnp.float32)
            for y in range(cy):
                line = jnp.broadcast_to(p_buf[t, x, pl.ds(y, 1), :], (rows, cz))
                got = jnp.take_along_axis(line, z_of, axis=1, mode="promise_in_bounds")
                cell_p = jnp.where(row_of == x * cy + y, got, cell_p)
            found.append(cell_p)
        while len(found) > 1:
            found = [sum(found[i : i + 2]) for i in range(0, len(found), 2)]
        return found[0]

    def scatter(flux):
        high = flux.astype(jnp.bfloat16).astype(jnp.float32)
        rest = flux - high
        mid = rest.astype(jnp.bfloat16).astype(jnp.float32)
        low = rest - mid
        pieces = []
        for s in range(rows):
            at_line = line_iota == jnp.broadcast_to(line_of[s : s + 1, :], line_iota.shape)
            pieces.append(
                jnp.concatenate(
                    [
                        jnp.where(at_line, jnp.broadcast_to(part[s : s + 1, :], at_line.shape), 0.0)
                        for part in (high, mid, low)
                    ],
                    axis=0,
                ).astype(jnp.bfloat16)
            )
        spread = jnp.dot(
            jnp.concatenate(pieces, axis=1), slot_column[...], preferred_element_type=jnp.float32
        )
        spread = spread[:lines] + spread[lines : 2 * lines] + spread[2 * lines :]
        return [
            spread[x % (cx // 2) * cy :][:cy, x // (cx // 2) * cz :][:, :cz] for x in range(cx)
        ]

    def halo_copy(t, side):
        src = (p_buf.at[t, 0], p_buf.at[t, cx - 1], y_stage.at[t, 0], y_stage.at[t, 1])[side]
        there = (has_w, has_e, has_s, has_n)[side].astype(jnp.int32)
        opposite = (EAST, WEST, NORTH, SOUTH)[side]
        lands = side + (opposite - side) * there
        return send(src, halo.at[t, lands], halo_send.at[t], halo_recv.at[t, lands],
                    partners[side])

    def send_x(t):
        halo_copy(t, WEST).start()
        halo_copy(t, EAST).start()

    def send_y(t):
        y_stage[t, 0] = p_buf[t, :, 0, :]
        y_stage[t, 1] = p_buf[t, :, cy - 1, :]
        halo_copy(t, SOUTH).start()
        halo_copy(t, NORTH).start()

    def wait_halo(t, side):
        send(halo.at[t, side], halo.at[t, side], halo_send.at[t],
             halo_recv.at[t, side], partners[side]).wait_recv()

    def all_cells(t):
        return send(cell_recv.at[t], cell_recv.at[t], cell_send.at[t], cell_rsem.at[t], along_x(1))

    def drain(t):
        send(halo.at[t], halo.at[t], halo_send.at[t], halo_recv.at[t, 0], partners[0]).wait_send()
        all_cells(t).wait_send()

    def cell_copy(t, d):
        return send(cell_buf.at[t], cell_recv.at[t, index_of[-d]],
                    cell_send.at[t], cell_rsem.at[t], along_x(d))

    def merge(t):
        cell_p = cell_buf[t]
        all_cells(t).wait_recv()
        for d in offsets:
            got = pltpu.roll(cell_recv[t, index_of[d]], (-d * wells) % rows, 0)
            cell_p = jnp.where(host == level + d, got, cell_p)
        return cell_p

    def well_step(seg, cell_p):
        before = pltpu.roll(seg, 1, 1)
        after = pltpu.roll(seg, cz - 1, 1)
        return 0.2 * seg + seg_inv * (rate + wi * cell_p + fm * before + fp * after)

    def grid_step(t, well_term, more):
        parts = []
        for x in range(cx):
            p = p_buf[t, x]
            total = 0.3 * p + coef[C_RHS, x] - coef[C_INV, x] * well_term[x]
            total += coef[C_U, x] * pltpu.roll(p, cz - 1, 1) + coef[C_D, x] * pltpu.roll(p, 1, 1)
            total += coef[C_N, x] * pltpu.roll(p, cy - 1, 0) + coef[C_S, x] * pltpu.roll(p, 1, 0)
            if x > 0:
                total += coef[C_W, x] * p_buf[t, x - 1]
            if x < cx - 1:
                total += coef[C_E, x] * p_buf[t, x + 1]
            parts.append(total)
        wait_halo(t, SOUTH)
        wait_halo(t, NORTH)
        for x in range(cx):
            north = jnp.broadcast_to(halo[t, NORTH, pl.ds(x, 1), :], (cy, cz))
            south = jnp.broadcast_to(halo[t, SOUTH, pl.ds(x, 1), :], (cy, cz))
            parts[x] += coef[C_EDGE, x] * jnp.where(sub == 0, south, north)
            if 0 < x < cx - 1:
                p_buf[t + 1, x] = parts[x]
        for side, x, at in ((WEST, 0, C_W), (EAST, cx - 1, C_E)):
            wait_halo(t, side)
            p_buf[t + 1, x] = parts[x] + coef[at, x] * halo[t, side]
            if more:
                halo_copy(t + 1, side).start()
        if more:
            send_y(t + 1)

    pl.when(has_w)(tx_copy().wait_recv)
    pl.when(has_s)(ty_copy().wait_recv)
    for x in range(cx):
        ex, ey, ez = tx_ref[x], ty_ref[x], tz_ref[x]
        wx = tx_halo[...] if x == 0 else tx_ref[x - 1]
        edge_y = jnp.broadcast_to(ty_halo[pl.ds(x, 1), :], (cy, cz))
        wy = jnp.where(sub == 0, edge_y, pltpu.roll(ey, 1, 0))
        wz = jnp.where(lane == 0, 0.0, pltpu.roll(ez, 1, 1))
        diag = acc_ref[x] + ex + wx + ey + wy + ez + wz
        inv = 0.7 / diag
        coef[C_W, x] = inv * wx
        coef[C_E, x] = jnp.where(has_e, inv * ex, 0.0) if x == cx - 1 else inv * ex
        coef[C_S, x] = jnp.where(sub == 0, 0.0, inv * wy)
        coef[C_N, x] = jnp.where(sub == cy - 1, 0.0, inv * ey)
        coef[C_EDGE, x] = jnp.where(
            sub == 0, inv * wy, jnp.where((sub == cy - 1) & has_n, inv * ey, 0.0)
        )
        coef[C_D, x] = inv * wz
        coef[C_U, x] = jnp.where(lane == cz - 1, 0.0, inv * ez)
        coef[C_INV, x] = inv
        coef[C_RHS, x] = inv * rhs_ref[x]

    for d in range(1, reach):
        pack_copy(d).wait_recv()
    for r in range(reach):
        for k in range(4):
            params[k, r * wells : (r + 1) * wells] = packs[r, k * wells : (k + 1) * wells]
    host = params[0]
    wi = params[1]
    rate = params[3]
    slot = lax.broadcasted_iota(jnp.int32, (rows, cz), 1)
    fm = jnp.where(slot > 0, params[2], 0.0)
    fp = jnp.where(slot < cz - 1, pltpu.roll(fm, cz - 1, 1), 0.0)
    seg_inv = 0.8 / (wi + fm + fp)
    mine = host == level

    seg = seg_inv * rate
    well_term = scatter(jnp.where(mine, -wi * seg, 0.0))
    for x in range(cx):
        p_buf[1, x] = coef[C_RHS, x] - coef[C_INV, x] * well_term[x]
    send_x(1)
    send_y(1)

    def sweep(t, seg, first):
        cell_p = gather(t)
        cell_buf[t] = cell_p
        if not first:
            seg = well_step(seg, merge(t - 1))
        flux = wi * (cell_p - well_step(seg, cell_p))
        well_term = scatter(jnp.where(mine, flux, 0.0))
        for d in offsets:
            cell_copy(t, d).start()
        return seg, well_term

    def middle(t, seg, first):
        seg, well_term = sweep(t, seg, first)
        if not first:
            drain(t - 1)
        grid_step(t, well_term, True)
        return seg

    seg = middle(1, seg, True)
    seg = lax.fori_loop(2, SWEEPS - 1, lambda t, seg: middle(t, seg, False), seg)
    last = SWEEPS - 1
    seg, well_term = sweep(last, seg, False)
    drain(last - 1)
    grid_step(last, well_term, False)
    p_copy = pltpu.make_async_copy(p_buf.at[SWEEPS], p_hbm, out_sem.at[0])
    p_copy.start()
    for d in range(1, reach):
        pack_copy(d).wait_send()
    pl.when(has_e)(lambda: tx_copy().wait_send())
    pl.when(has_n)(lambda: ty_copy().wait_send())
    drain(last)
    seg = well_step(seg, merge(last))
    s_out[0] = seg[:wells]
    s_copy = pltpu.make_async_copy(s_out, s_hbm, out_sem.at[1])
    s_copy.start()
    p_copy.wait()
    s_copy.wait()


def hand_out(p_in, s_in, p_out, s_out, p_held, s_held, sems):
    arrays = ((p_in, p_held, p_out), (s_in, s_held, s_out))
    inward = [pltpu.make_async_copy(a, b, sems.at[0, i]) for i, (a, b, _) in enumerate(arrays)]
    outward = [pltpu.make_async_copy(b, c, sems.at[1, i]) for i, (_, b, c) in enumerate(arrays)]
    for copy in inward:
        copy.start()
    for fetched, copy in zip(inward, outward):
        fetched.wait()
        copy.start()
    for copy in outward:
        copy.wait()


def shards(*args):
    rhs, acc, tx, ty, tz, held, host, wi, sc, sr = args
    reach = held.shape[0]
    wells, slots = wi.shape[1:]
    rows = reach * wells
    cx, cy, cz = rhs.shape
    peers = 2 * (reach - 1)
    hbm = pl.BlockSpec(memory_space=pltpu.HBM)
    f32 = jnp.float32
    shapes = (jax.ShapeDtypeStruct(rhs.shape, f32), jax.ShapeDtypeStruct(sr.shape, f32))
    swept = pl.pallas_call(
        functools.partial(kernel, reach),
        out_shape=shapes,
        in_specs=[hbm] * 10,
        out_specs=(hbm, hbm),
        scratch_shapes=[pltpu.VMEM(a.shape, a.dtype) for a in args]
        + [
            pltpu.SemaphoreType.DMA((len(args),)),
            pltpu.VMEM(sr.shape, f32),
            pltpu.SemaphoreType.DMA((2,)),
            pltpu.VMEM((SWEEPS + 1, cx, cy, cz), f32),
            pltpu.VMEM((SWEEPS, 4, cy, cz), f32),
            pltpu.VMEM((SWEEPS, 2, cx, cz), f32),
            pltpu.VMEM((9, cx, cy, cz), f32),
            pltpu.VMEM((cy, cz), f32),
            pltpu.VMEM((cx, cz), f32),
            pltpu.VMEM((cx, cz), f32),
            pltpu.VMEM((reach, 4 * wells, slots), f32),
            pltpu.VMEM((4, rows, slots), f32),
            pltpu.VMEM((rows, slots), jnp.int32),
            pltpu.VMEM((rows * slots, 2 * cz), jnp.bfloat16),
            pltpu.VMEM((SWEEPS, rows, slots), f32),
            pltpu.VMEM((SWEEPS, peers, rows, slots), f32),
            pltpu.SemaphoreType.DMA((reach + 1,)),
            pltpu.SemaphoreType.DMA((reach + 1,)),
            pltpu.SemaphoreType.DMA((SWEEPS,)),
            pltpu.SemaphoreType.DMA((SWEEPS, 4)),
            pltpu.SemaphoreType.DMA((SWEEPS,)),
            pltpu.SemaphoreType.DMA((SWEEPS,)),
        ],
        compiler_params=pltpu.CompilerParams(
            collective_id=0, has_side_effects=True, vmem_limit_bytes=60 * 1024 * 1024
        ),
    )(*args)
    return pl.pallas_call(
        hand_out,
        out_shape=shapes,
        in_specs=[hbm] * 2,
        out_specs=(hbm, hbm),
        scratch_shapes=[
            pltpu.VMEM(rhs.shape, f32),
            pltpu.VMEM(sr.shape, f32),
            pltpu.SemaphoreType.DMA((2, 2)),
        ],
        compiler_params=pltpu.CompilerParams(vmem_limit_bytes=60 * 1024 * 1024),
    )(*swept)


def solution(mesh):
    return jax.shard_map(
        shards,
        mesh=mesh,
        in_specs=(P("gx", "gy", None),) * 5
        + (P(None, "gx", "gy", None),)
        + (P("gx", "gy", None),) * 4,
        out_specs=(P("gx", "gy", None), P("gx", "gy", None)),
        check_vma=False,
    )
```
